256 devices in a mesh: dom: 16 (over x, z_hi), shot: 16 (over y, z_lo, core).
Axes of the slice: x: 4, y: 4, z: 8 (z_hi: 4, z_lo: 2; z = z_hi * 2 + z_lo), core: 2. Of those that a mesh axis runs over, the one named last changes fastest.
Arguments:
- fwd_later: float32 [32, 3, 62608], P('shot', None, 'dom'), may hold values from -6 to 6, as said below
- fwd_now: float32 [32, 3, 62608], P('shot', None, 'dom'), may hold values from -6 to 6, as said below
- adj_later: float32 [32, 3, 62608], P('shot', None, 'dom'), may hold values from -6 to 6, as said below
- adj_now: float32 [32, 3, 62608], P('shot', None, 'dom'), may hold values from -6 to 6, as said below
- adj_src: bfloat16 [32, 3, 62608], P('shot', None, 'dom'), may hold values from -12 to 12, as said below
- mass_step: float32 [62608], P('dom'), may hold values from 0.02 to 0.05, as said below
- shear_mod: float32 [1792], P('dom'), may hold values from 0.5 to 2
- lame_mod: float32 [1792], P('dom'), may hold values from 0.5 to 2
- stiffness: bfloat16 [2, 192, 192], replicated, may hold values from -0.2 to 2.5, as said below
- conn: int32 [1792, 64], P('dom'), may hold values from 0 to 3912, as said below
- face_nodes: int32 [16, 2, 559], P('dom'), may hold values from 0 to 3912, as said below
- face_count: int32 [16, 2], P('dom'), may hold values from 0 to 559, as said below
Outputs:
- fwd_out: bfloat16 [32, 3, 62608], P('shot', None, 'dom')
- adj_out: bfloat16 [32, 3, 62608], P('shot', None, 'dom')
- model_grad: float32 [2, 1792], P(None, 'dom')
The draws below stay inside these ranges and needn't reach their ends.
Inputs may be any that keep to these rules, and one draw needn't show every extreme that they name: `conn`: each row lists one element's nodes as block-local numbers in the order of its 4 x 4 x 4 node lattice (first lattice direction slowest); elements of a block share the nodes of common faces, edges and corners. `face_nodes`: slot k of the upper face list of block d and slot k of the lower face list of block d + 1 name the same physical node; the lists of a block are disjoint. face_count[d, 1] equals face_count[d + 1, 0] and is a multiple of 43; the lower count of the first block and the upper count of the last are 0; some pair of blocks shares all 559 slots. `fwd_later`: copies of a shared face node hold equal values in both blocks. `fwd_now`: copies of a shared face node hold equal values in both blocks. `adj_later`: copies of a shared face node hold equal values in both blocks. `adj_now`: copies of a shared face node hold equal values in both blocks. `adj_src`: copies of a shared face node hold equal values in both blocks. `mass_step`: copies of a shared face node hold equal values in both blocks. `stiffness`: each tile is symmetric.
All inputs are finite; a program needn't handle non-finite values.
Results may differ from the reference program's by a relative error of at most 0.0041.
Values sent between devices are 32-bit elements; how exact they have to be, the bound alone decides.
A program may use at most 128 MiB of HBM per device.

```python
import math
import jax
import jax.numpy as jnp
from jax import lax

ELEM_X = 2
ELEM_Y = 4
ELEM_Z = 14
SHOT_DEV = 2
STEPS = 2
COMP = 3
NPE = 64
TILE = 192
ELEM_DEV = 112
NODES_DEV = 3913
FACE = 559
ELEMS = 1792
NODES = 62608
SHOTS = 32


def face_geometry(key):
    blocks = ELEMS // ELEM_DEV
    nodes_x = 3 * ELEM_X + 1
    nodes_y = 3 * ELEM_Y + 1
    nodes_z = 3 * ELEM_Z + 1
    perm_keys = jax.random.split(jax.random.fold_in(key, 11), blocks)
    labels = jax.vmap(lambda one_key: jax.random.permutation(one_key, NODES_DEV))(perm_keys).astype(jnp.int32)
    elem_id = jnp.arange(ELEM_DEV)
    elem_xpos = elem_id // (ELEM_Y * ELEM_Z)
    elem_ypos = elem_id // ELEM_Z % ELEM_Y
    elem_zpos = elem_id % ELEM_Z
    corner = jnp.arange(NPE)
    off_xpos = corner // 16
    off_ypos = corner // 4 % 4
    off_zpos = corner % 4
    lattice = (3 * elem_xpos[:, None] + off_xpos[None, :]) * (nodes_y * nodes_z)
    lattice = lattice + (3 * elem_ypos[:, None] + off_ypos[None, :]) * nodes_z
    lattice = lattice + 3 * elem_zpos[:, None] + off_zpos[None, :]
    conn = labels[:, lattice].reshape(blocks * ELEM_DEV, NPE)
    face_slot = jnp.arange(FACE)
    left_side = labels[:, face_slot]
    right_side = labels[:, (nodes_x - 1) * nodes_y * nodes_z + face_slot]
    nodes_face = jnp.stack([left_side, right_side], axis=1)
    heights = jax.random.randint(jax.random.fold_in(key, 12), (blocks - 1,), (nodes_y + 1) // 2, nodes_y + 1)
    chosen = jax.random.randint(jax.random.fold_in(key, 13), (), 0, blocks - 1)
    heights = jnp.where(jnp.arange(blocks - 1) == chosen, nodes_y, heights)
    shared = (heights * nodes_z).astype(jnp.int32)
    nothing = jnp.zeros((1,), jnp.int32)
    counts = jnp.stack([jnp.concatenate([nothing, shared]), jnp.concatenate([shared, nothing])], axis=1)
    return (conn.astype(jnp.int32), nodes_face.astype(jnp.int32), counts.astype(jnp.int32))


def tie_faces(key, field):
    conn, nodes_face, counts = face_geometry(key)
    blocks = ELEMS // ELEM_DEV
    shaped = field.reshape(field.shape[:-1] + (blocks, NODES_DEV))
    block_id = jnp.broadcast_to(jnp.arange(blocks)[:, None], (blocks, FACE))
    earlier = (block_id - 1) % blocks
    left_side = nodes_face[:, 0]
    right_before = nodes_face[(jnp.arange(blocks) - 1) % blocks, 1]
    incoming = shaped[..., earlier, right_before]
    present = shaped[..., block_id, left_side]
    inside = jnp.arange(FACE)[None, :] < counts[:, 0][:, None]
    joined = jnp.where(inside, incoming, present)
    shaped = shaped.at[..., block_id, left_side].set(joined)
    return shaped.reshape(field.shape)


def drawn_field(key, salt, scale):
    sub = jax.random.fold_in(key, salt)
    raw = jax.random.normal(sub, (SHOTS, COMP, NODES), jnp.float32) * scale
    return jnp.clip(raw, -6.0 * scale, 6.0 * scale)


def draw_fwd_later(key, part):
    raw = drawn_field(key, 21, 1.0)
    return tie_faces(key, raw)


def draw_fwd_now(key, part):
    raw = drawn_field(key, 22, 1.0)
    return tie_faces(key, raw)


def draw_adj_later(key, part):
    raw = drawn_field(key, 23, 1.0)
    return tie_faces(key, raw)


def draw_adj_now(key, part):
    raw = drawn_field(key, 24, 1.0)
    return tie_faces(key, raw)


def draw_adj_src(key, part):
    raw = drawn_field(key, 25, 2.0)
    return tie_faces(key, raw).astype(jnp.bfloat16)


def draw_mass_step(key, part):
    sub = jax.random.fold_in(key, 26)
    raw = jnp.exp(jax.random.uniform(sub, (NODES,), jnp.float32, math.log(0.02), math.log(0.05)))
    return tie_faces(key, raw)


def draw_stiffness(key, part):
    sub = jax.random.fold_in(key, 31)
    noise = jnp.clip(jax.random.normal(sub, (2, TILE, TILE), jnp.float32), -4.0, 4.0)
    noise = noise * (0.5 / math.sqrt(TILE))
    symmetric = (noise + jnp.swapaxes(noise, 1, 2)) * 0.7071
    diagonal = jax.random.uniform(jax.random.fold_in(sub, 1), (2, TILE), jnp.float32, 1.5, 2.5)
    identity = jnp.eye(TILE, dtype=jnp.float32)
    tiles = symmetric * (1.0 - identity) + diagonal[:, :, None] * identity
    return tiles.astype(jnp.bfloat16)


def draw_conn(key, part):
    conn, nodes_face, counts = face_geometry(key)
    return conn


def draw_face_nodes(key, part):
    conn, nodes_face, counts = face_geometry(key)
    return nodes_face


def draw_face_count(key, part):
    conn, nodes_face, counts = face_geometry(key)
    return counts


def block_levels(key, extent, pieces, smallest, top_value):
    def one(axis_at, shards_of):
        steps = jax.random.uniform(jax.random.fold_in(jax.random.fold_in(key, 6), axis_at), (shards_of,), jnp.float32, smallest / len(pieces), top_value / len(pieces))
        return jnp.repeat(jnp.exp(steps), extent[axis_at] // shards_of).reshape((-1,) + (1,) * (len(extent) - axis_at - 1))

    level = one(*pieces[0])
    for cut in pieces[1:]:
        level = level * one(*cut)
    return level


def setup_inputs(seed: int = 0) -> dict:
    streams_of = jax.random.split(jax.random.key(seed), 13)
    fwd_later = draw_fwd_later(jax.random.fold_in(streams_of[12], 71), 0)
    fwd_now = draw_fwd_now(jax.random.fold_in(streams_of[12], 71), 0)
    adj_later = draw_adj_later(jax.random.fold_in(streams_of[12], 71), 0)
    adj_now = draw_adj_now(jax.random.fold_in(streams_of[12], 71), 0)
    adj_src = draw_adj_src(jax.random.fold_in(streams_of[12], 71), 0)
    mass_step = draw_mass_step(jax.random.fold_in(streams_of[12], 71), 0)
    shear_mod = jnp.clip(jnp.exp(math.log(2.0) - 1.3862944 * jax.random.uniform(streams_of[6], (ELEMS,), jnp.float32) ** block_levels(streams_of[6], (ELEMS,), ((0, 16),), -0.2, 0.2)), 0.5, 2.0)
    lame_mod = jnp.clip(jnp.exp(math.log(2.0) - 1.3862944 * jax.random.uniform(streams_of[7], (ELEMS,), jnp.float32) ** block_levels(streams_of[7], (ELEMS,), ((0, 16),), -0.2, 0.2)), 0.5, 2.0)
    stiffness = draw_stiffness(jax.random.fold_in(streams_of[12], 71), 0)
    conn = draw_conn(jax.random.fold_in(streams_of[12], 71), 0)
    face_nodes = draw_face_nodes(jax.random.fold_in(streams_of[12], 71), 0)
    face_count = draw_face_count(jax.random.fold_in(streams_of[12], 71), 0)
    return dict(fwd_later=fwd_later, fwd_now=fwd_now, adj_later=adj_later, adj_now=adj_now, adj_src=adj_src, mass_step=mass_step, shear_mod=shear_mod, lame_mod=lame_mod, stiffness=stiffness, conn=conn, face_nodes=face_nodes, face_count=face_count)


def element_pass(fields, conn_block, shear_block, lame_block, tiles_joined):
    count_fields = fields.shape[0]
    count_elems = conn_block.shape[0]
    flat = conn_block.reshape(-1)
    gathered = fields.astype(jnp.bfloat16)[:, :, flat].reshape(count_fields, COMP, count_elems, NPE)
    wide = gathered.astype(jnp.float32)
    products = jnp.einsum('fcen,cnk->fek', wide, tiles_joined)
    elem_force = shear_block[None, :, None] * products[:, :, :TILE] + lame_block[None, :, None] * products[:, :, TILE:]
    spread = jnp.transpose(elem_force.reshape(count_fields, count_elems, COMP, NPE), (0, 2, 1, 3)).reshape(count_fields, COMP, count_elems * NPE)
    forces = jnp.zeros(fields.shape, jnp.float32).at[:, :, flat].add(spread)
    half = count_fields // 2
    forward = products[:half].reshape(half, count_elems, 2, COMP, NPE)
    grads = jnp.einsum('scen,sepcn->pe', wide[half:], forward)
    return (forces, grads)

def couple_faces(forces, face_nodes, face_count):
    blocks = forces.shape[2]
    slots = jnp.arange(FACE)
    block_rows = jnp.broadcast_to(jnp.arange(blocks)[:, None], (blocks, FACE))
    left_nodes = face_nodes[:, 0]
    right_nodes = face_nodes[:, 1]
    mask_left = jnp.where(slots[None, :] < face_count[:, 0:1], 1.0, 0.0).astype(jnp.float32)
    mask_right = jnp.where(slots[None, :] < face_count[:, 1:2], 1.0, 0.0).astype(jnp.float32)
    out_left = forces[:, :, block_rows, left_nodes] * mask_left
    out_right = forces[:, :, block_rows, right_nodes] * mask_right
    zero_row = jnp.zeros_like(out_left[:, :, :1])
    from_left = jnp.concatenate([zero_row, out_right[:, :, :-1]], axis=2)
    from_right = jnp.concatenate([out_left[:, :, 1:], zero_row], axis=2)
    forces = forces.at[:, :, block_rows, left_nodes].add(from_left * mask_left)
    forces = forces.at[:, :, block_rows, right_nodes].add(from_right * mask_right)
    return forces

def run_group(packed, mass_step, shear_mod, lame_mod, tiles_joined, conn, face_nodes, face_count):
    fwd_later, fwd_now, adj_later, adj_now, adj_src = packed
    shots_here = fwd_now.shape[0]
    count_fields = 2 * shots_here
    blocks = NODES // NODES_DEV
    later_state = jnp.concatenate([fwd_later, adj_later], axis=0)
    now_state = jnp.concatenate([fwd_now, adj_now], axis=0)
    source = mass_step[None, None, :] * adj_src.astype(jnp.float32)
    conn_blocks = conn.reshape(blocks, ELEM_DEV, NPE)
    shear_blocks = shear_mod.reshape(blocks, ELEM_DEV)
    lame_blocks = lame_mod.reshape(blocks, ELEM_DEV)
    grad_total = jnp.zeros((2, ELEMS), jnp.float32)

    def per_block(inputs):
        return element_pass(inputs[0], inputs[1], inputs[2], inputs[3], tiles_joined)
    for instant in range(STEPS):
        now_blocks = jnp.moveaxis(now_state.reshape(count_fields, COMP, blocks, NODES_DEV), 2, 0)
        forces, grads = lax.map(per_block, (now_blocks, conn_blocks, shear_blocks, lame_blocks))
        forces = jnp.moveaxis(forces, 0, 2)
        forces = couple_faces(forces, face_nodes, face_count).reshape(count_fields, COMP, NODES)
        grad_total = grad_total + jnp.moveaxis(grads, 0, 1).reshape(2, ELEMS)
        earlier = 2.0 * now_state - later_state - mass_step[None, None, :] * forces
        earlier = earlier.at[shots_here:].add(source)
        later_state = now_state
        now_state = earlier
    return (now_state[:shots_here], now_state[shots_here:], grad_total)

def reference(fwd_later, fwd_now, adj_later, adj_now, adj_src, mass_step, shear_mod, lame_mod, stiffness, conn, face_nodes, face_count):
    tiles_joined = jnp.concatenate([stiffness[0], stiffness[1]], axis=1).astype(jnp.float32).reshape(COMP, NPE, 2 * TILE)
    groups = SHOTS // SHOT_DEV

    def regroup(field):
        return field.reshape(groups, SHOT_DEV, COMP, NODES)
    packed = (regroup(fwd_later), regroup(fwd_now), regroup(adj_later), regroup(adj_now), regroup(adj_src))

    def one_group(group_fields):
        return run_group(group_fields, mass_step, shear_mod, lame_mod, tiles_joined, conn, face_nodes, face_count)
    fwd_final, adj_final, grads = lax.map(one_group, packed)
    scale = -1.0 / (16.0 * math.sqrt(SHOTS))
    model_grad = lax.optimization_barrier(jnp.sum(grads, axis=0)) * scale
    fwd_out = fwd_final.reshape(SHOTS, COMP, NODES).astype(jnp.bfloat16)
    adj_out = adj_final.reshape(SHOTS, COMP, NODES).astype(jnp.bfloat16)
    return (fwd_out, adj_out, model_grad)
```

```python
import functools
import math

import jax
import jax.numpy as jnp
from jax import lax
from jax.experimental import pallas as pl
from jax.experimental.pallas import tpu as pltpu
from jax.sharding import PartitionSpec as P

STEPS = 2
COMP = 3
NPE = 64
TILE = 192
FIELDS = 4
CH = 16
LO = 256
HI = 16
EL = 128
FP = 640
F32 = jnp.float32
BF16 = jnp.bfloat16
MESH = pl.DeviceIdType.MESH
NT = (((1,), (1,)), ((), ()))


def rotated(me, step, size):
    return lax.rem(me + step, size)


def pick(rows, table):
    out = table[:CH]
    for hi in range(1, HI):
        out = jnp.where(rows == hi, table[hi * CH : (hi + 1) * CH], out)
    return out


def kernel(
    doms,
    inner,
    outer,
    nodes,
    scale,
    fl_ref,
    fn_ref,
    al_ref,
    an_ref,
    src_ref,
    mass_ref,
    shear_ref,
    lame_ref,
    stiff_ref,
    conn_ref,
    faces_ref,
    count_ref,
    fwd_ref,
    adj_ref,
    grad_ref,
    now_s,
    later_s,
    src_s,
    mass_s,
    hi_s,
    lo_s,
    fhi_s,
    flo_s,
    oh_s,
    ohf_s,
    gath_s,
    gmat_s,
    force_s,
    lhs_s,
    lhsf_s,
    send_s,
    recv_s,
    shear_s,
    lame_s,
    gsend_s,
    gin_s,
    gmid_s,
    gout_s,
    face_send,
    face_recv,
    in_send,
    in_recv,
    out_send,
    out_recv,
):
    dom = lax.axis_index("dom")
    shot = lax.axis_index("shot")
    mine_in = lax.rem(shot, inner)
    mine_out = lax.div(shot, inner)
    up = {"dom": rotated(dom, 1, doms)}
    down = {"dom": rotated(dom, doms - 1, doms)}
    near = [{"shot": mine_out * inner + rotated(mine_in, r, inner)} for r in range(1, inner)]
    far = [{"shot": rotated(mine_out, r, outer) * inner + mine_in} for r in range(1, outer)]

    barrier = pltpu.get_barrier_semaphore()
    peers = [up, down, *near, *far]
    for peer in peers:
        pl.semaphore_signal(barrier, inc=1, device_id=peer, device_id_type=MESH)

    elems = conn_ref.shape[1]
    slots = faces_ref.shape[1]

    hi_s[...] = jnp.full(hi_s.shape, -1, jnp.int32)
    lo_s[...] = jnp.full(lo_s.shape, -1, jnp.int32)
    fhi_s[...] = jnp.full(fhi_s.shape, -1, jnp.int32)
    flo_s[...] = jnp.full(flo_s.shape, -1, jnp.int32)
    conn = conn_ref[...]
    hi_s[:, :elems] = lax.shift_right_logical(conn, 8)
    lo_s[:, :elems] = lax.bitwise_and(conn, 255)
    slot = lax.broadcasted_iota(jnp.int32, (1, slots), 1)
    for side in range(2):
        face = faces_ref[side : side + 1, :]
        inside = slot < count_ref[0:1, side : side + 1]
        fhi_s[side : side + 1, :slots] = jnp.where(inside, lax.shift_right_logical(face, 8), -1)
        flo_s[side : side + 1, :slots] = jnp.where(inside, lax.bitwise_and(face, 255), -1)

    place = lax.broadcasted_iota(jnp.int32, (LO, EL), 0)

    def build(n, carry):
        lanes = pl.ds(pl.multiple_of(n * EL, EL), EL)
        oh_s[:, lanes] = jnp.where(place == lo_s[pl.ds(n, 1), :], 1.0, 0.0).astype(BF16)
        return carry

    lax.fori_loop(0, NPE, build, 0, unroll=4)
    for q in range(2 * FP // EL):
        side, at = divmod(q * EL, FP)
        row = flo_s[side : side + 1, at : at + EL]
        ohf_s[:, q * EL : (q + 1) * EL] = jnp.where(place == row, 1.0, 0.0).astype(BF16)

    now_s[...] = jnp.zeros(now_s.shape, F32)
    later_s[...] = jnp.zeros(later_s.shape, F32)
    src_s[...] = jnp.zeros(src_s.shape, F32)
    mass_s[...] = jnp.zeros(mass_s.shape, F32)
    force_s[...] = jnp.zeros(force_s.shape, F32)
    shear_s[...] = jnp.zeros(shear_s.shape, F32)
    lame_s[...] = jnp.zeros(lame_s.shape, F32)
    shear_s[:, :elems] = shear_ref[...]
    lame_s[:, :elems] = lame_ref[...]
    spans = [(hi, hi * LO, min(LO, nodes - hi * LO)) for hi in range(HI)]
    for hi, at, width in spans:
        part = mass_ref[0:1, at : at + width]
        mass_s[hi * CH : (hi + 1) * CH, :width] = jnp.broadcast_to(part, (CH, width))
        for c in range(COMP):
            row = hi * CH + c * FIELDS
            now_s[row : row + 2, :width] = fn_ref[c, :, at : at + width]
            now_s[row + 2 : row + 4, :width] = an_ref[c, :, at : at + width]
            later_s[row : row + 2, :width] = fl_ref[c, :, at : at + width]
            later_s[row + 2 : row + 4, :width] = al_ref[c, :, at : at + width]
            src_s[row + 2 : row + 4, :width] = src_ref[c, :, at : at + width].astype(F32)
    src_s[...] = src_s[...] * mass_s[...]

    shear = shear_s[...]
    lame = lame_s[...]
    grads = [jnp.zeros((1, EL), F32), jnp.zeros((1, EL), F32)]
    copies = []
    for step in range(STEPS):
        state = now_s[...].astype(BF16)

        def gather(m, carry):
            lanes = pl.ds(pl.multiple_of(m * 2 * EL, 2 * EL), 2 * EL)
            table = jnp.dot(state, oh_s[:, lanes], preferred_element_type=F32)
            rows = jnp.concatenate(
                [hi_s[pl.ds(2 * m, 1), :], hi_s[pl.ds(2 * m + 1, 1), :]], axis=1
            )
            got = pick(jnp.broadcast_to(rows, (CH, 2 * EL)), table)
            first = pl.multiple_of(m * 2 * CH, 2 * CH)
            gath_s[pl.ds(first, CH), :] = got[:, :EL]
            gath_s[pl.ds(first + CH, CH), :] = got[:, EL:]
            return carry

        lax.fori_loop(0, NPE // 2, gather, 0, unroll=2)
        for c in range(COMP):
            for f in range(FIELDS):
                part = gath_s[pl.ds(c * FIELDS + f, NPE, stride=CH), :]
                gmat_s[c * NPE : (c + 1) * NPE, f * EL : (f + 1) * EL] = part.astype(BF16)

        stiff = stiff_ref[...]
        for half in range(2):
            prod = jnp.dot(
                stiff, gmat_s[:, half * 2 * EL : (half + 1) * 2 * EL], preferred_element_type=F32
            )
            if half == 0:
                other = gmat_s[:, 2 * EL :].astype(F32)
                for p in range(2):
                    both = jnp.sum(other * prod[p * TILE : (p + 1) * TILE], axis=0, keepdims=True)
                    grads[p] = grads[p] + both[:, :EL] + both[:, EL:]
            for s in range(2):
                f = half * 2 + s
                cols = slice(s * EL, (s + 1) * EL)
                total = shear * prod[:TILE, cols] + lame * prod[TILE:, cols]
                for c in range(COMP):
                    first = (c * FIELDS + f) * NPE
                    force_s[first : first + NPE, :] = total[c * NPE : (c + 1) * NPE]

        if step == STEPS - 1:
            gsend_s[...] = jnp.zeros(gsend_s.shape, F32)
            gsend_s[0:1, :] = grads[0]
            gsend_s[1:2, :] = grads[1]
            gin_s[0] = gsend_s[...]
            if step == 0:
                pl.semaphore_wait(barrier, len(peers))
            in_copies = [
                pltpu.make_async_remote_copy(
                    src_ref=gsend_s,
                    dst_ref=gin_s.at[r],
                    send_sem=in_send.at[r],
                    recv_sem=in_recv.at[r],
                    device_id=near[r - 1],
                    device_id_type=MESH,
                )
                for r in range(1, inner)
            ]
            for copy in in_copies:
                copy.start()

        def spread(n, carry):
            lanes = pl.ds(pl.multiple_of(n * EL, EL), EL)
            part = force_s[pl.ds(n, CH, stride=NPE), :]
            rows = jnp.broadcast_to(hi_s[pl.ds(n, 1), :], (CH, EL))
            for hi in range(HI):
                lhs_s[hi * CH : (hi + 1) * CH, lanes] = jnp.where(rows == hi, part, 0.0).astype(BF16)
            return carry

        lax.fori_loop(0, NPE, spread, 0, unroll=2)
        forces = lax.dot_general(lhs_s[...], oh_s[...], NT, preferred_element_type=F32)

        rounded = forces.astype(BF16)
        for b in range(FP // EL):
            table = jnp.dot(
                rounded, ohf_s[:, b * 2 * EL : (b + 1) * 2 * EL], preferred_element_type=F32
            )
            for h in range(2):
                side, at = divmod((2 * b + h) * EL, FP)
                row = fhi_s[side : side + 1, at : at + EL]
                got = pick(jnp.broadcast_to(row, (CH, EL)), table[:, h * EL : (h + 1) * EL])
                send_s[step, side, :, at : at + EL] = got

        if step == 0:
            pl.semaphore_wait(barrier, len(peers))
        here = [
            pltpu.make_async_remote_copy(
                src_ref=send_s.at[step, side],
                dst_ref=recv_s.at[step, 1 - side],
                send_sem=face_send.at[step, side],
                recv_sem=face_recv.at[step, 1 - side],
                device_id=(down, up)[side],
                device_id_type=MESH,
            )
            for side in range(2)
        ]
        for copy in here:
            copy.start()

        now = now_s[...]
        mass = mass_s[...]
        ahead = 2.0 * now - later_s[...] - mass * forces + src_s[...]
        later_s[...] = now
        now_s[...] = ahead

        if step == STEPS - 1:
            for copy in in_copies:
                copy.wait()
            total = gin_s[lax.rem(mine_in, inner)]
            for i in range(1, inner):
                total = total + gin_s[rotated(mine_in, inner - i, inner)]
            gmid_s[...] = total
            gout_s[0] = total
            out_copies = [
                pltpu.make_async_remote_copy(
                    src_ref=gmid_s,
                    dst_ref=gout_s.at[r],
                    send_sem=out_send.at[r],
                    recv_sem=out_recv.at[r],
                    device_id=far[r - 1],
                    device_id_type=MESH,
                )
                for r in range(1, outer)
            ]
            for copy in out_copies:
                copy.start()

        for copy in here:
            copy.wait()
        for q in range(2 * FP // EL):
            side, at = divmod(q * EL, FP)
            part = recv_s[step, side, :, at : at + EL]
            rows = jnp.broadcast_to(fhi_s[side : side + 1, at : at + EL], (CH, EL))
            for hi in range(HI):
                lhsf_s[hi * CH : (hi + 1) * CH, q * EL : (q + 1) * EL] = jnp.where(
                    rows == hi, part, 0.0
                ).astype(BF16)
        joined = lax.dot_general(lhsf_s[...], ohf_s[...], NT, preferred_element_type=F32)
        now_s[...] = now_s[...] - mass_s[...] * joined

    for hi, at, width in spans:
        for c in range(COMP):
            row = hi * CH + c * FIELDS
            fwd_ref[c, :, at : at + width] = now_s[row : row + 2, :width].astype(BF16)
            adj_ref[c, :, at : at + width] = now_s[row + 2 : row + 4, :width].astype(BF16)

    for copy in out_copies:
        copy.wait()
    total = gout_s[lax.rem(mine_out, outer)]
    for i in range(1, outer):
        total = total + gout_s[rotated(mine_out, outer - i, outer)]
    grad_ref[...] = (total * scale)[:2, :elems]


def local(
    doms,
    shots,
    fwd_later,
    fwd_now,
    adj_later,
    adj_now,
    adj_src,
    mass_step,
    shear_mod,
    lame_mod,
    stiffness,
    conn,
    face_nodes,
    face_count,
):
    fields, comps, nodes = fwd_now.shape
    elems = conn.shape[0]
    inner = math.gcd(shots, 4)
    outer = shots // inner
    turn = lambda x: jnp.transpose(x, (1, 0, 2))
    scale = -1.0 / (16.0 * math.sqrt(fields * shots))
    dma = pltpu.SemaphoreType.DMA
    vmem = pltpu.VMEM
    body = functools.partial(kernel, doms, inner, outer, nodes, scale)
    fwd, adj, grad = pl.pallas_call(
        body,
        out_shape=(
            jax.ShapeDtypeStruct((comps, fields, nodes), BF16),
            jax.ShapeDtypeStruct((comps, fields, nodes), BF16),
            jax.ShapeDtypeStruct((2, elems), F32),
        ),
        in_specs=[pl.BlockSpec(memory_space=pltpu.VMEM)] * 12,
        out_specs=[pl.BlockSpec(memory_space=pltpu.VMEM)] * 3,
        scratch_shapes=[
            vmem((HI * CH, LO), F32),
            vmem((HI * CH, LO), F32),
            vmem((HI * CH, LO), F32),
            vmem((HI * CH, LO), F32),
            vmem((NPE, EL), jnp.int32),
            vmem((NPE, EL), jnp.int32),
            vmem((2, FP), jnp.int32),
            vmem((2, FP), jnp.int32),
            vmem((LO, NPE * EL), BF16),
            vmem((LO, 2 * FP), BF16),
            vmem((NPE * CH, EL), F32),
            vmem((TILE, FIELDS * EL), BF16),
            vmem((CH * NPE, EL), F32),
            vmem((HI * CH, NPE * EL), BF16),
            vmem((HI * CH, 2 * FP), BF16),
            vmem((STEPS, 2, CH, FP), F32),
            vmem((STEPS, 2, CH, FP), F32),
            vmem((1, EL), F32),
            vmem((1, EL), F32),
            vmem((8, EL), F32),
            vmem((inner, 8, EL), F32),
            vmem((8, EL), F32),
            vmem((outer, 8, EL), F32),
            dma((STEPS, 2)),
            dma((STEPS, 2)),
            dma((inner,)),
            dma((inner,)),
            dma((outer,)),
            dma((outer,)),
        ],
        compiler_params=pltpu.CompilerParams(
            collective_id=0, has_side_effects=True, vmem_limit_bytes=40 * 2**20
        ),
        name="fwi_window",
    )(
        turn(fwd_later),
        turn(fwd_now),
        turn(adj_later),
        turn(adj_now),
        turn(adj_src),
        mass_step[None],
        shear_mod[None],
        lame_mod[None],
        stiffness.reshape(2 * TILE, TILE),
        conn.T,
        face_nodes[0],
        face_count,
    )
    return turn(fwd), turn(adj), grad


def solution(mesh):
    in_specs = (
        P("shot", None, "dom"),
        P("shot", None, "dom"),
        P("shot", None, "dom"),
        P("shot", None, "dom"),
        P("shot", None, "dom"),
        P("dom"),
        P("dom"),
        P("dom"),
        P(),
        P("dom", None),
        P("dom", None, None),
        P("dom", None),
    )
    out_specs = (P("shot", None, "dom"), P("shot", None, "dom"), P(None, "dom"))
    return jax.shard_map(
        functools.partial(local, mesh.shape["dom"], mesh.shape["shot"]),
        mesh=mesh,
        in_specs=in_specs,
        out_specs=out_specs,
        check_vma=False,
    )
```

```python
import functools
import math

import jax
import jax.numpy as jnp
from jax import lax
from jax.experimental import pallas as pl
from jax.experimental.pallas import tpu as pltpu
from jax.sharding import PartitionSpec as P

STEPS = 2
COMP = 3
NPE = 64
TILE = 192
CH = 8
LO = 256
HI = 16
EL = 128
FQ = 5
GROUPS = NPE + 2 * FQ
ROWS = 80
WIDE = 8
F32 = jnp.float32
BF16 = jnp.bfloat16
MESH = pl.DeviceIdType.MESH


def rotated(me, step, size):
    return lax.rem(me + step, size)


def rows_of(ref, first, count):
    return jnp.concatenate(
        [jnp.broadcast_to(ref[pl.ds(first + k, 1), :], (CH, EL)) for k in range(count)], axis=1
    )


def pick(rows, table):
    out = table[:CH]
    for hi in range(1, HI):
        out = jnp.where(rows == hi, table[hi * CH : (hi + 1) * CH], out)
    return out


def place(rows, part):
    return jnp.concatenate([jnp.where(rows == hi, part, 0.0) for hi in range(HI)], axis=0).astype(BF16)


def kernel(
    doms,
    inner,
    outer,
    nodes,
    scale,
    fl_h,
    fn_h,
    al_h,
    an_h,
    src_h,
    mass_h,
    shear_h,
    lame_h,
    stiff_h,
    conn_h,
    faces_h,
    count_h,
    fwd_ref,
    adj_ref,
    grad_ref,
    fl_v,
    fn_v,
    al_v,
    an_v,
    src_v,
    mass_v,
    shear_v,
    lame_v,
    stiff_v,
    conn_v,
    faces_v,
    count_v,
    load_sem,
    now_s,
    later_s,
    src_s,
    mass_s,
    hi_s,
    lo_s,
    oh_s,
    oht_s,
    gath_s,
    gmat_s,
    prod_s,
    force_s,
    lhs_s,
    lhsf_s,
    send_s,
    recv_s,
    mod_s,
    gsend_s,
    gin_s,
    gmid_s,
    gout_s,
    face_send,
    face_recv,
    in_send,
    in_recv,
    out_send,
    out_recv,
):
    names = ("conn", "faces", "count", "fn", "an", "stiff", "shear", "lame", "fl", "al", "mass", "src")
    from_hbm = (conn_h, faces_h, count_h, fn_h, an_h, stiff_h, shear_h, lame_h, fl_h, al_h, mass_h, src_h)
    to_vmem = (conn_v, faces_v, count_v, fn_v, an_v, stiff_v, shear_v, lame_v, fl_v, al_v, mass_v, src_v)
    loads = {
        name: pltpu.make_async_copy(a, b, load_sem.at[i])
        for i, (name, a, b) in enumerate(zip(names, from_hbm, to_vmem))
    }
    for load in loads.values():
        load.start()

    dom = lax.axis_index("dom")
    shot = lax.axis_index("shot")
    mine_in = lax.rem(shot, inner)
    mine_out = lax.div(shot, inner)
    below = dom > 0
    above = dom < doms - 1
    ways = ({"dom": rotated(dom, doms - 1, doms)}, {"dom": rotated(dom, 1, doms)})
    near = [{"shot": mine_out * inner + rotated(mine_in, r, inner)} for r in range(1, inner)]
    far = [{"shot": rotated(mine_out, r, outer) * inner + mine_in} for r in range(1, outer)]

    barrier = pltpu.get_barrier_semaphore()
    for there, way in zip((below, above), ways):

        @pl.when(there)
        def _():
            pl.semaphore_signal(barrier, inc=1, device_id=way, device_id_type=MESH)

    for peer in (*near, *far):
        pl.semaphore_signal(barrier, inc=1, device_id=peer, device_id_type=MESH)
    greeted = inner + outer - 2 + jnp.where(below, 1, 0) + jnp.where(above, 1, 0)

    def face_copy(step, half, side):
        return pltpu.make_async_remote_copy(
            src_ref=send_s.at[step, half, side],
            dst_ref=recv_s.at[step, half, 1 - side],
            send_sem=face_send.at[step, half, side],
            recv_sem=face_recv.at[step, half, 1 - side],
            device_id=ways[side],
            device_id_type=MESH,
        )

    now_s[...] = jnp.zeros(now_s.shape, F32)
    later_s[...] = jnp.zeros(later_s.shape, F32)
    src_s[...] = jnp.zeros(src_s.shape, F32)
    mass_s[...] = jnp.zeros(mass_s.shape, F32)
    force_s[...] = jnp.zeros(force_s.shape, F32)
    mod_s[...] = jnp.zeros(mod_s.shape, F32)
    hi_s[...] = jnp.full(hi_s.shape, -1, jnp.int32)
    lo_s[...] = jnp.full(lo_s.shape, -1, jnp.int32)

    elems = conn_v.shape[1]
    slots = faces_v.shape[1]
    loads["conn"].wait()
    conn = conn_v[...]
    hi_s[:NPE, :elems] = lax.shift_right_logical(conn, 8)
    lo_s[:NPE, :elems] = lax.bitwise_and(conn, 255)
    loads["faces"].wait()
    loads["count"].wait()
    slot = lax.broadcasted_iota(jnp.int32, (1, EL), 1)
    for side in range(2):
        for q in range(FQ):
            width = min(EL, slots - q * EL)
            row = NPE + side * FQ + q
            face = faces_v[side : side + 1, q * EL : q * EL + width]
            inside = slot[:, :width] + q * EL < count_v[0:1, side : side + 1]
            hi_s[row : row + 1, :width] = jnp.where(inside, lax.shift_right_logical(face, 8), -1)
            lo_s[row : row + 1, :width] = jnp.where(inside, lax.bitwise_and(face, 255), -1)

    spot = lax.broadcasted_iota(jnp.int32, (LO, 2 * EL), 0)

    def build(m, carry):
        lanes = pl.ds(pl.multiple_of(m * 2 * EL, 2 * EL), 2 * EL)
        row = jnp.concatenate([lo_s[pl.ds(2 * m, 1), :], lo_s[pl.ds(2 * m + 1, 1), :]], axis=1)
        oh_s[:, lanes] = jnp.where(spot == row, 1.0, 0.0).astype(BF16)
        return carry

    lax.fori_loop(0, GROUPS // 2, build, 0, unroll=2)
    turned = jnp.concatenate([lo_s[...], jnp.full((EL - ROWS, EL), -1, jnp.int32)], axis=0).T
    across = lax.broadcasted_iota(jnp.int32, (EL, LO), 1)
    for n in range(GROUPS):
        column = jnp.broadcast_to(turned[:, n : n + 1], (EL, LO))
        oht_s[n * EL : (n + 1) * EL, :] = jnp.where(across == column, 1.0, 0.0).astype(BF16)

    spans = [(hi, hi * LO, min(LO, nodes - hi * LO)) for hi in range(HI)]

    def fill(ref, half, block):
        for hi, at, width in spans:
            for c in range(COMP):
                row = hi * CH + 2 * c
                ref[half, row : row + 2, :width] = block[c, :, at : at + width].astype(F32)

    loads["fn"].wait()
    fill(now_s, 0, fn_v)
    loads["an"].wait()
    fill(now_s, 1, an_v)
    loads["stiff"].wait()
    loads["shear"].wait()
    loads["lame"].wait()
    mod_s[0:1, :elems] = shear_v[...]
    mod_s[1:2, :elems] = lame_v[...]
    stiff = stiff_v[...]
    shear = mod_s[0:1, :]
    lame = mod_s[1:2, :]
    shear = jnp.concatenate([shear, shear], axis=1)
    lame = jnp.concatenate([lame, lame], axis=1)
    grads = [jnp.zeros((1, EL), F32), jnp.zeros((1, EL), F32)]

    near_copies = [
        pltpu.make_async_remote_copy(
            src_ref=gsend_s,
            dst_ref=gin_s.at[r],
            send_sem=in_send.at[r],
            recv_sem=in_recv.at[r],
            device_id=near[r - 1],
            device_id_type=MESH,
        )
        for r in range(1, inner)
    ]
    far_copies = [
        pltpu.make_async_remote_copy(
            src_ref=gmid_s,
            dst_ref=gout_s.at[r],
            send_sem=out_send.at[r],
            recv_sem=out_recv.at[r],
            device_id=far[r - 1],
            device_id_type=MESH,
        )
        for r in range(1, outer)
    ]

    def compute(step, half, grads):
        state = now_s[half].astype(BF16)
        table = jnp.dot(state, oh_s[:, : NPE * EL], preferred_element_type=F32)
        for n in range(0, NPE, WIDE):
            got = pick(rows_of(hi_s, n, WIDE), table[:, n * EL : (n + WIDE) * EL])
            for k in range(WIDE):
                gath_s[(n + k) * CH : (n + k + 1) * CH, :] = got[:, k * EL : (k + 1) * EL]
        for c in range(COMP):
            both = [gath_s[pl.ds(2 * c + s, NPE, stride=CH), :] for s in range(2)]
            gmat_s[c * NPE : (c + 1) * NPE, :] = jnp.concatenate(both, axis=1).astype(BF16)
        prod = jnp.dot(stiff, gmat_s[...], preferred_element_type=F32)
        total = shear * prod[:TILE] + lame * prod[TILE:]
        for c in range(COMP):
            for s in range(2):
                first = (2 * c + s) * NPE
                force_s[first : first + NPE, :] = total[c * NPE : (c + 1) * NPE, s * EL : (s + 1) * EL]
        if half == 0:
            prod_s[...] = prod
        else:
            other = gmat_s[...].astype(F32)
            for p in range(2):
                both = jnp.sum(other * prod_s[p * TILE : (p + 1) * TILE, :], axis=0, keepdims=True)
                grads[p] = grads[p] + both[:, :EL] + both[:, EL:]
            if step == STEPS - 1:
                gsend_s[...] = jnp.zeros(gsend_s.shape, F32)
                gsend_s[0:1, :] = grads[0]
                gsend_s[1:2, :] = grads[1]
                for copy in near_copies:
                    copy.start()

        def spread(m, carry):
            lanes = pl.ds(pl.multiple_of(m * 2 * EL, 2 * EL), 2 * EL)
            part = [force_s[pl.ds(2 * m + k, CH, stride=NPE), :] for k in range(2)]
            lhs_s[:, lanes] = place(rows_of(hi_s, 2 * m, 2), jnp.concatenate(part, axis=1))
            return carry

        lax.fori_loop(0, NPE // 2, spread, 0, unroll=4)
        forces = jnp.dot(lhs_s[...], oht_s[: NPE * EL, :], preferred_element_type=F32)

        table = jnp.dot(
            forces.astype(BF16), oh_s[:, NPE * EL : GROUPS * EL], preferred_element_type=F32
        )
        for side in range(2):
            first = side * FQ
            got = pick(
                rows_of(hi_s, NPE + first, FQ), table[:, first * EL : (first + FQ) * EL]
            )
            send_s[step, half, side] = got
        if step == 0 and half == 0:
            pl.semaphore_wait(barrier, greeted)
        for side, there in enumerate((below, above)):

            @pl.when(there)
            def _():
                face_copy(step, half, side).start()

        return forces

    def advance(half, forces):
        now = now_s[half]
        ahead = 2.0 * now - later_s[half] - mass_s[...] * forces
        if half == 1:
            ahead = ahead + src_s[...]
        later_s[half] = now
        now_s[half] = ahead

    def join(step, half):
        for side, there in enumerate((below, above)):

            @pl.when(there)
            def _():
                face_copy(step, half, 1 - side).wait_recv()

        for side in range(2):
            first = side * FQ
            lhsf_s[:, first * EL : (first + FQ) * EL] = place(
                rows_of(hi_s, NPE + first, FQ), recv_s[step, half, side]
            )
        joined = jnp.dot(lhsf_s[...], oht_s[NPE * EL : GROUPS * EL, :], preferred_element_type=F32)
        now_s[half] = now_s[half] - mass_s[...] * joined

    def write(half, out):
        for hi, at, width in spans:
            for c in range(COMP):
                row = hi * CH + 2 * c
                out[c, :, at : at + width] = now_s[half, row : row + 2, :width].astype(BF16)

    forces = compute(0, 0, grads)
    loads["fl"].wait()
    fill(later_s, 0, fl_v)
    loads["al"].wait()
    fill(later_s, 1, al_v)
    loads["mass"].wait()
    for hi, at, width in spans:
        part = mass_v[at : at + width]
        mass_s[hi * CH : (hi + 1) * CH, :width] = jnp.broadcast_to(part[None], (CH, width))
    loads["src"].wait()
    for hi, at, width in spans:
        for c in range(COMP):
            row = hi * CH + 2 * c
            src_s[row : row + 2, :width] = src_v[c, :, at : at + width].astype(F32)
    src_s[...] = src_s[...] * mass_s[...]
    advance(0, forces)
    advance(1, compute(0, 1, grads))
    for step in range(1, STEPS):
        for half in range(2):
            join(step - 1, half)
            advance(half, compute(step, half, grads))
    last = STEPS - 1

    for copy in near_copies:
        copy.wait()
    gin_s[0] = gsend_s[...]
    total = gin_s[mine_in]
    for i in range(1, inner):
        total = total + gin_s[rotated(mine_in, inner - i, inner)]
    gmid_s[...] = total
    for copy in far_copies:
        copy.start()

    join(last, 0)
    write(0, fwd_ref)
    join(last, 1)
    write(1, adj_ref)

    for copy in far_copies:
        copy.wait()
    gout_s[0] = gmid_s[...]
    total = gout_s[mine_out]
    for i in range(1, outer):
        total = total + gout_s[rotated(mine_out, outer - i, outer)]
    grad_ref[...] = (total * scale)[:2, :elems]
    for step in range(STEPS):
        for half in range(2):
            for side, there in enumerate((below, above)):

                @pl.when(there)
                def _():
                    face_copy(step, half, side).wait_send()


def local(
    doms,
    shots,
    fwd_later,
    fwd_now,
    adj_later,
    adj_now,
    adj_src,
    mass_step,
    shear_mod,
    lame_mod,
    stiffness,
    conn,
    face_nodes,
    face_count,
):
    fields, comps, nodes = fwd_now.shape
    elems = conn.shape[0]
    inner = math.gcd(shots, 4)
    outer = shots // inner
    turn = lambda x: jnp.transpose(x, (1, 0, 2))
    scale = -1.0 / (16.0 * math.sqrt(fields * shots))
    dma = pltpu.SemaphoreType.DMA
    vmem = pltpu.VMEM
    body = functools.partial(kernel, doms, inner, outer, nodes, scale)
    operands = (
        turn(fwd_later),
        turn(fwd_now),
        turn(adj_later),
        turn(adj_now),
        turn(adj_src),
        mass_step,
        shear_mod[None],
        lame_mod[None],
        stiffness.reshape(2 * TILE, TILE),
        conn.T,
        face_nodes[0],
        face_count,
    )
    half = (2, HI * CH, LO)
    fwd, adj, grad = pl.pallas_call(
        body,
        out_shape=(
            jax.ShapeDtypeStruct((comps, fields, nodes), BF16),
            jax.ShapeDtypeStruct((comps, fields, nodes), BF16),
            jax.ShapeDtypeStruct((2, elems), F32),
        ),
        in_specs=[pl.BlockSpec(memory_space=pltpu.HBM)] * 12,
        out_specs=[pl.BlockSpec(memory_space=pltpu.VMEM)] * 3,
        scratch_shapes=[
            *[vmem(x.shape, x.dtype) for x in operands],
            dma((len(operands),)),
            vmem(half, F32),
            vmem(half, F32),
            vmem(half[1:], F32),
            vmem(half[1:], F32),
            vmem((ROWS, EL), jnp.int32),
            vmem((ROWS, EL), jnp.int32),
            vmem((LO, GROUPS * EL), BF16),
            vmem((GROUPS * EL, LO), BF16),
            vmem((NPE * CH, EL), F32),
            vmem((TILE, 2 * EL), BF16),
            vmem((2 * TILE, 2 * EL), F32),
            vmem((CH * NPE, EL), F32),
            vmem((HI * CH, NPE * EL), BF16),
            vmem((HI * CH, 2 * FQ * EL), BF16),
            vmem((STEPS, 2, 2, CH, FQ * EL), F32),
            vmem((STEPS, 2, 2, CH, FQ * EL), F32),
            vmem((8, EL), F32),
            vmem((8, EL), F32),
            vmem((inner, 8, EL), F32),
            vmem((8, EL), F32),
            vmem((outer, 8, EL), F32),
            dma((STEPS, 2, 2)),
            dma((STEPS, 2, 2)),
            dma((inner,)),
            dma((inner,)),
            dma((outer,)),
            dma((outer,)),
        ],
        compiler_params=pltpu.CompilerParams(
            collective_id=0, has_side_effects=True, vmem_limit_bytes=56 * 2**20
        ),
        name="fwi_window",
    )(*operands)
    return turn(fwd), turn(adj), grad


def solution(mesh):
    in_specs = (
        P("shot", None, "dom"),
        P("shot", None, "dom"),
        P("shot", None, "dom"),
        P("shot", None, "dom"),
        P("shot", None, "dom"),
        P("dom"),
        P("dom"),
        P("dom"),
        P(),
        P("dom", None),
        P("dom", None, None),
        P("dom", None),
    )
    out_specs = (P("shot", None, "dom"), P("shot", None, "dom"), P(None, "dom"))
    return jax.shard_map(
        functools.partial(local, mesh.shape["dom"], mesh.shape["shot"]),
        mesh=mesh,
        in_specs=in_specs,
        out_specs=out_specs,
        check_vma=False,
    )
```

```python
import functools
import math

import jax
import jax.numpy as jnp
from jax import lax
from jax.experimental import pallas as pl
from jax.experimental.pallas import tpu as pltpu
from jax.sharding import PartitionSpec as P

STEPS = 2
COMP = 3
NPE = 64
TILE = 192
CH = 8
LO = 256
HI = 16
EL = 128
FQ = 5
GROUPS = NPE + 2 * FQ
ROWS = 80
WIDE = 8
F32 = jnp.float32
BF16 = jnp.bfloat16
MESH = pl.DeviceIdType.MESH


def rotated(me, step, size):
    return lax.rem(me + step, size)


def rows_of(ref, first, count):
    return jnp.concatenate(
        [jnp.broadcast_to(ref[pl.ds(first + k, 1), :], (CH, EL)) for k in range(count)], axis=1
    )


def pick(rows, table):
    out = table[:CH]
    for hi in range(1, HI):
        out = jnp.where(rows == hi, table[hi * CH : (hi + 1) * CH], out)
    return out


def place(rows, part):
    return jnp.concatenate([jnp.where(rows == hi, part, 0.0) for hi in range(HI)], axis=0).astype(BF16)


def kernel(
    doms,
    inner,
    outer,
    nodes,
    scale,
    fl_h,
    fn_h,
    al_h,
    an_h,
    src_h,
    mass_h,
    shear_h,
    lame_h,
    stiff_h,
    conn_h,
    faces_h,
    count_h,
    fwd_ref,
    adj_ref,
    grad_ref,
    fl_v,
    fn_v,
    al_v,
    an_v,
    src_v,
    mass_v,
    shear_v,
    lame_v,
    stiff_v,
    conn_v,
    faces_v,
    count_v,
    load_sem,
    now_s,
    later_s,
    src_s,
    mass_s,
    hi_s,
    lo_s,
    oh_s,
    oht_s,
    gath_s,
    gmat_s,
    prod_s,
    force_s,
    lhsf_s,
    send_s,
    recv_s,
    mod_s,
    gsend_s,
    gin_s,
    gmid_s,
    gout_s,
    face_send,
    face_recv,
    in_send,
    in_recv,
    out_send,
    out_recv,
):
    names = ("conn", "faces", "count", "fn", "an", "stiff", "shear", "lame", "fl", "al", "mass", "src")
    from_hbm = (conn_h, faces_h, count_h, fn_h, an_h, stiff_h, shear_h, lame_h, fl_h, al_h, mass_h, src_h)
    to_vmem = (conn_v, faces_v, count_v, fn_v, an_v, stiff_v, shear_v, lame_v, fl_v, al_v, mass_v, src_v)
    loads = {
        name: pltpu.make_async_copy(a, b, load_sem.at[i])
        for i, (name, a, b) in enumerate(zip(names, from_hbm, to_vmem))
    }
    for load in loads.values():
        load.start()

    dom = lax.axis_index("dom")
    shot = lax.axis_index("shot")
    mine_in = lax.rem(shot, inner)
    mine_out = lax.div(shot, inner)
    below = dom > 0
    above = dom < doms - 1
    ways = ({"dom": rotated(dom, doms - 1, doms)}, {"dom": rotated(dom, 1, doms)})
    near = [{"shot": mine_out * inner + rotated(mine_in, r, inner)} for r in range(1, inner)]
    far = [{"shot": rotated(mine_out, r, outer) * inner + mine_in} for r in range(1, outer)]

    barrier = pltpu.get_barrier_semaphore()
    for there, way in zip((below, above), ways):

        @pl.when(there)
        def _():
            pl.semaphore_signal(barrier, inc=1, device_id=way, device_id_type=MESH)

    for peer in (*near, *far):
        pl.semaphore_signal(barrier, inc=1, device_id=peer, device_id_type=MESH)
    greeted = inner + outer - 2 + jnp.where(below, 1, 0) + jnp.where(above, 1, 0)

    def face_copy(step, half, side):
        return pltpu.make_async_remote_copy(
            src_ref=send_s.at[step, half, side],
            dst_ref=recv_s.at[step, half, 1 - side],
            send_sem=face_send.at[step, half, side],
            recv_sem=face_recv.at[step, half, 1 - side],
            device_id=ways[side],
            device_id_type=MESH,
        )

    now_s[...] = jnp.zeros(now_s.shape, F32)
    later_s[...] = jnp.zeros(later_s.shape, F32)
    src_s[...] = jnp.zeros(src_s.shape, F32)
    mass_s[...] = jnp.zeros(mass_s.shape, F32)
    force_s[...] = jnp.zeros(force_s.shape, F32)
    mod_s[...] = jnp.zeros(mod_s.shape, F32)
    hi_s[...] = jnp.full(hi_s.shape, -1, jnp.int32)
    lo_s[...] = jnp.full(lo_s.shape, -1, jnp.int32)

    elems = conn_v.shape[1]
    slots = faces_v.shape[1]
    loads["conn"].wait()
    conn = conn_v[...]
    hi_s[:NPE, :elems] = lax.shift_right_logical(conn, 8)
    lo_s[:NPE, :elems] = lax.bitwise_and(conn, 255)
    loads["faces"].wait()
    loads["count"].wait()
    slot = lax.broadcasted_iota(jnp.int32, (1, EL), 1)
    for side in range(2):
        for q in range(FQ):
            width = min(EL, slots - q * EL)
            row = NPE + side * FQ + q
            face = faces_v[side : side + 1, q * EL : q * EL + width]
            inside = slot[:, :width] + q * EL < count_v[0:1, side : side + 1]
            hi_s[row : row + 1, :width] = jnp.where(inside, lax.shift_right_logical(face, 8), -1)
            lo_s[row : row + 1, :width] = jnp.where(inside, lax.bitwise_and(face, 255), -1)

    spot = lax.broadcasted_iota(jnp.int32, (LO, 2 * EL), 0)

    def build(m, carry):
        lanes = pl.ds(pl.multiple_of(m * 2 * EL, 2 * EL), 2 * EL)
        row = jnp.concatenate([lo_s[pl.ds(2 * m, 1), :], lo_s[pl.ds(2 * m + 1, 1), :]], axis=1)
        oh_s[:, lanes] = jnp.where(spot == row, 1.0, 0.0).astype(BF16)
        return carry

    lax.fori_loop(0, GROUPS // 2, build, 0, unroll=2)

    def turn_blocks(first, last):
        for m in range(first, last):
            part = slice(m * 2 * EL, (m + 1) * 2 * EL)
            oht_s[part, :] = oh_s[:, part].T

    spans = [(hi, hi * LO, min(LO, nodes - hi * LO)) for hi in range(HI)]

    def fill(ref, half, block):
        for hi, at, width in spans:
            for c in range(COMP):
                row = hi * CH + 2 * c
                ref[half, row : row + 2, :width] = block[c, :, at : at + width].astype(F32)

    loads["fn"].wait()
    fill(now_s, 0, fn_v)
    loads["an"].wait()
    fill(now_s, 1, an_v)
    loads["stiff"].wait()
    loads["shear"].wait()
    loads["lame"].wait()
    mod_s[0:1, :elems] = shear_v[...]
    mod_s[1:2, :elems] = lame_v[...]
    stiff = stiff_v[...]
    shear = mod_s[0:1, :]
    lame = mod_s[1:2, :]
    shear = jnp.concatenate([shear, shear], axis=1)
    lame = jnp.concatenate([lame, lame], axis=1)
    grads = [jnp.zeros((1, EL), F32), jnp.zeros((1, EL), F32)]

    near_copies = [
        pltpu.make_async_remote_copy(
            src_ref=gsend_s,
            dst_ref=gin_s.at[r],
            send_sem=in_send.at[r],
            recv_sem=in_recv.at[r],
            device_id=near[r - 1],
            device_id_type=MESH,
        )
        for r in range(1, inner)
    ]
    far_copies = [
        pltpu.make_async_remote_copy(
            src_ref=gmid_s,
            dst_ref=gout_s.at[r],
            send_sem=out_send.at[r],
            recv_sem=out_recv.at[r],
            device_id=far[r - 1],
            device_id_type=MESH,
        )
        for r in range(1, outer)
    ]

    def compute(step, half, grads):
        state = now_s[half].astype(BF16)
        table = jnp.dot(state, oh_s[:, : NPE * EL], preferred_element_type=F32)
        for n in range(0, NPE, WIDE):
            got = pick(rows_of(hi_s, n, WIDE), table[:, n * EL : (n + WIDE) * EL])
            for k in range(WIDE):
                gath_s[(n + k) * CH : (n + k + 1) * CH, :] = got[:, k * EL : (k + 1) * EL]
            if step == 0 and half == 0:
                quarter = GROUPS // 4
                turn_blocks(n * quarter // NPE, (n + WIDE) * quarter // NPE)
        for c in range(COMP):
            both = [gath_s[pl.ds(2 * c + s, NPE, stride=CH), :] for s in range(2)]
            gmat_s[c * NPE : (c + 1) * NPE, :] = jnp.concatenate(both, axis=1).astype(BF16)
        prod = jnp.dot(stiff, gmat_s[...], preferred_element_type=F32)
        total = shear * prod[:TILE] + lame * prod[TILE:]
        for c in range(COMP):
            for s in range(2):
                first = (2 * c + s) * NPE
                force_s[first : first + NPE, :] = total[c * NPE : (c + 1) * NPE, s * EL : (s + 1) * EL]
        if half == 0:
            prod_s[...] = prod
        else:
            other = gmat_s[...].astype(F32)
            for p in range(2):
                both = jnp.sum(other * prod_s[p * TILE : (p + 1) * TILE, :], axis=0, keepdims=True)
                grads[p] = grads[p] + both[:, :EL] + both[:, EL:]
            if step == STEPS - 1:
                gsend_s[...] = jnp.zeros(gsend_s.shape, F32)
                gsend_s[0:1, :] = grads[0]
                gsend_s[1:2, :] = grads[1]
                for copy in near_copies:
                    copy.start()

        def spread(n):
            part = [force_s[pl.ds(n + k, CH, stride=NPE), :] for k in range(2)]
            return place(rows_of(hi_s, n, 2), jnp.concatenate(part, axis=1))

        lhs = jnp.concatenate([spread(n) for n in range(0, NPE, 2)], axis=1)
        if step == 0 and half == 0:
            turn_blocks(GROUPS // 4, GROUPS // 2)
        forces = jnp.dot(lhs, oht_s[: NPE * EL, :], preferred_element_type=F32)

        table = jnp.dot(
            forces.astype(BF16), oh_s[:, NPE * EL : GROUPS * EL], preferred_element_type=F32
        )
        for side in range(2):
            first = side * FQ
            got = pick(
                rows_of(hi_s, NPE + first, FQ), table[:, first * EL : (first + FQ) * EL]
            )
            send_s[step, half, side] = got
        if step == 0 and half == 0:
            pl.semaphore_wait(barrier, greeted)
        for side, there in enumerate((below, above)):

            @pl.when(there)
            def _():
                face_copy(step, half, side).start()

        return forces

    def advance(half, forces):
        now = now_s[half]
        ahead = 2.0 * now - later_s[half] - mass_s[...] * forces
        if half == 1:
            ahead = ahead + src_s[...]
        later_s[half] = now
        now_s[half] = ahead

    def join(step, half):
        for side, there in enumerate((below, above)):

            @pl.when(there)
            def _():
                face_copy(step, half, 1 - side).wait_recv()

        for side in range(2):
            first = side * FQ
            lhsf_s[:, first * EL : (first + FQ) * EL] = place(
                rows_of(hi_s, NPE + first, FQ), recv_s[step, half, side]
            )
        joined = jnp.dot(lhsf_s[...], oht_s[NPE * EL : GROUPS * EL, :], preferred_element_type=F32)
        now_s[half] = now_s[half] - mass_s[...] * joined

    def write(half, out):
        for hi, at, width in spans:
            for c in range(COMP):
                row = hi * CH + 2 * c
                out[c, :, at : at + width] = now_s[half, row : row + 2, :width].astype(BF16)

    forces = compute(0, 0, grads)
    loads["fl"].wait()
    fill(later_s, 0, fl_v)
    loads["al"].wait()
    fill(later_s, 1, al_v)
    loads["mass"].wait()
    for hi, at, width in spans:
        part = mass_v[at : at + width]
        mass_s[hi * CH : (hi + 1) * CH, :width] = jnp.broadcast_to(part[None], (CH, width))
    loads["src"].wait()
    for hi, at, width in spans:
        for c in range(COMP):
            row = hi * CH + 2 * c
            src_s[row : row + 2, :width] = src_v[c, :, at : at + width].astype(F32)
    src_s[...] = src_s[...] * mass_s[...]
    advance(0, forces)
    advance(1, compute(0, 1, grads))
    for step in range(1, STEPS):
        for half in range(2):
            join(step - 1, half)
            advance(half, compute(step, half, grads))
    last = STEPS - 1

    for copy in near_copies:
        copy.wait()
    gin_s[0] = gsend_s[...]
    total = gin_s[mine_in]
    for i in range(1, inner):
        total = total + gin_s[rotated(mine_in, inner - i, inner)]
    gmid_s[...] = total
    for copy in far_copies:
        copy.start()

    join(last, 0)
    write(0, fwd_ref)
    join(last, 1)
    write(1, adj_ref)

    for copy in far_copies:
        copy.wait()
    gout_s[0] = gmid_s[...]
    total = gout_s[mine_out]
    for i in range(1, outer):
        total = total + gout_s[rotated(mine_out, outer - i, outer)]
    grad_ref[...] = (total * scale)[:2, :elems]
    for step in range(STEPS):
        for half in range(2):
            for side, there in enumerate((below, above)):

                @pl.when(there)
                def _():
                    face_copy(step, half, side).wait_send()


def put(fwd_ref, adj_ref, grad_ref, fwd_out, adj_out, grad_out, fwd_v, adj_v, grad_v, sem):
    rows = ((fwd_ref, fwd_v, fwd_out), (adj_ref, adj_v, adj_out), (grad_ref, grad_v, grad_out))
    ins = [pltpu.make_async_copy(a, v, sem.at[i]) for i, (a, v, b) in enumerate(rows)]
    outs = [pltpu.make_async_copy(v, b, sem.at[3 + i]) for i, (a, v, b) in enumerate(rows)]
    for copy in ins:
        copy.start()
    for copy, out in zip(ins, outs):
        copy.wait()
        out.start()
    for out in outs:
        out.wait()


def local(
    doms,
    shots,
    fwd_later,
    fwd_now,
    adj_later,
    adj_now,
    adj_src,
    mass_step,
    shear_mod,
    lame_mod,
    stiffness,
    conn,
    face_nodes,
    face_count,
):
    fields, comps, nodes = fwd_now.shape
    elems = conn.shape[0]
    inner = math.gcd(shots, 4)
    outer = shots // inner
    turn = lambda x: jnp.transpose(x, (1, 0, 2))
    scale = -1.0 / (16.0 * math.sqrt(fields * shots))
    dma = pltpu.SemaphoreType.DMA
    vmem = pltpu.VMEM
    body = functools.partial(kernel, doms, inner, outer, nodes, scale)
    operands = (
        turn(fwd_later),
        turn(fwd_now),
        turn(adj_later),
        turn(adj_now),
        turn(adj_src),
        mass_step,
        shear_mod[None],
        lame_mod[None],
        stiffness.reshape(2 * TILE, TILE),
        conn.T,
        face_nodes[0],
        face_count,
    )
    half = (2, HI * CH, LO)
    fwd, adj, grad = pl.pallas_call(
        body,
        out_shape=(
            jax.ShapeDtypeStruct((comps, fields, nodes), BF16),
            jax.ShapeDtypeStruct((comps, fields, nodes), BF16),
            jax.ShapeDtypeStruct((2, elems), F32),
        ),
        in_specs=[pl.BlockSpec(memory_space=pltpu.HBM)] * 12,
        out_specs=[pl.BlockSpec(memory_space=pltpu.VMEM)] * 3,
        scratch_shapes=[
            *[vmem(x.shape, x.dtype) for x in operands],
            dma((len(operands),)),
            vmem(half, F32),
            vmem(half, F32),
            vmem(half[1:], F32),
            vmem(half[1:], F32),
            vmem((ROWS, EL), jnp.int32),
            vmem((ROWS, EL), jnp.int32),
            vmem((LO, GROUPS * EL), BF16),
            vmem((GROUPS * EL, LO), BF16),
            vmem((NPE * CH, EL), F32),
            vmem((TILE, 2 * EL), BF16),
            vmem((2 * TILE, 2 * EL), F32),
            vmem((CH * NPE, EL), F32),
            vmem((HI * CH, 2 * FQ * EL), BF16),
            vmem((STEPS, 2, 2, CH, FQ * EL), F32),
            vmem((STEPS, 2, 2, CH, FQ * EL), F32),
            vmem((8, EL), F32),
            vmem((8, EL), F32),
            vmem((inner, 8, EL), F32),
            vmem((8, EL), F32),
            vmem((outer, 8, EL), F32),
            dma((STEPS, 2, 2)),
            dma((STEPS, 2, 2)),
            dma((inner,)),
            dma((inner,)),
            dma((outer,)),
            dma((outer,)),
        ],
        compiler_params=pltpu.CompilerParams(
            collective_id=0, has_side_effects=True, vmem_limit_bytes=56 * 2**20
        ),
        name="fwi_window",
    )(*operands)
    whole = (fwd, adj, grad)
    fwd, adj, grad = pl.pallas_call(
        put,
        out_shape=tuple(jax.ShapeDtypeStruct(x.shape, x.dtype) for x in whole),
        in_specs=[pl.BlockSpec(memory_space=pl.ANY)] * 3,
        out_specs=[pl.BlockSpec(memory_space=pl.ANY)] * 3,
        scratch_shapes=[*[vmem(x.shape, x.dtype) for x in whole], dma((6,))],
        compiler_params=pltpu.CompilerParams(vmem_limit_bytes=56 * 2**20),
        name="results",
    )(*whole)
    return turn(fwd), turn(adj), grad


def solution(mesh):
    in_specs = (
        P("shot", None, "dom"),
        P("shot", None, "dom"),
        P("shot", None, "dom"),
        P("shot", None, "dom"),
        P("shot", None, "dom"),
        P("dom"),
        P("dom"),
        P("dom"),
        P(),
        P("dom", None),
        P("dom", None, None),
        P("dom", None),
    )
    out_specs = (P("shot", None, "dom"), P("shot", None, "dom"), P(None, "dom"))
    return jax.shard_map(
        functools.partial(local, mesh.shape["dom"], mesh.shape["shot"]),
        mesh=mesh,
        in_specs=in_specs,
        out_specs=out_specs,
        check_vma=False,
    )
```

```python
import functools
import math

import jax
import jax.numpy as jnp
from jax import lax
from jax.experimental import pallas as pl
from jax.experimental.pallas import tpu as pltpu
from jax.sharding import PartitionSpec as P

STEPS = 2
COMP = 3
NPE = 64
TILE = 192
CH = 8
LO = 256
HI = 16
EL = 128
FQ = 5
GROUPS = NPE + 2 * FQ
ROWS = 80
WIDE = 8
BATCH = 32
TURNS = 9
F32 = jnp.float32
BF16 = jnp.bfloat16
MESH = pl.DeviceIdType.MESH


def rotated(me, step, size):
    return lax.rem(me + step, size)


def rows_of(ref, first, count):
    return jnp.concatenate(
        [jnp.broadcast_to(ref[pl.ds(first + k, 1), :], (CH, EL)) for k in range(count)], axis=1
    )


def pick(rows, table):
    out = table[:CH]
    for hi in range(1, HI):
        out = jnp.where(rows == hi, table[hi * CH : (hi + 1) * CH], out)
    return out


def place(rows, part):
    return jnp.concatenate([jnp.where(rows == hi, part, 0.0) for hi in range(HI)], axis=0).astype(BF16)


def kernel(
    doms,
    inner,
    outer,
    nodes,
    scale,
    fl_h,
    fn_h,
    al_h,
    an_h,
    src_h,
    mass_h,
    shear_h,
    lame_h,
    stiff_h,
    conn_h,
    faces_h,
    count_h,
    fwd_ref,
    adj_ref,
    grad_ref,
    fl_v,
    fn_v,
    al_v,
    an_v,
    src_v,
    mass_v,
    shear_v,
    lame_v,
    stiff_v,
    conn_v,
    faces_v,
    count_v,
    load_sem,
    now_s,
    later_s,
    src_s,
    mass_s,
    hi_s,
    lo_s,
    oh_s,
    oht_s,
    gath_s,
    gmat_s,
    prod_s,
    force_s,
    lhsf_s,
    made_s,
    send_s,
    recv_s,
    mod_s,
    gsend_s,
    gin_s,
    gmid_s,
    gout_s,
    face_send,
    face_recv,
    in_send,
    in_recv,
    out_send,
    out_recv,
):
    names = ("conn", "faces", "count", "fn", "an", "stiff", "shear", "lame", "fl", "al", "mass", "src")
    from_hbm = (conn_h, faces_h, count_h, fn_h, an_h, stiff_h, shear_h, lame_h, fl_h, al_h, mass_h, src_h)
    to_vmem = (conn_v, faces_v, count_v, fn_v, an_v, stiff_v, shear_v, lame_v, fl_v, al_v, mass_v, src_v)
    loads = {
        name: pltpu.make_async_copy(a, b, load_sem.at[i])
        for i, (name, a, b) in enumerate(zip(names, from_hbm, to_vmem))
    }
    for load in loads.values():
        load.start()

    dom = lax.axis_index("dom")
    shot = lax.axis_index("shot")
    mine_in = lax.rem(shot, inner)
    mine_out = lax.div(shot, inner)
    below = dom > 0
    above = dom < doms - 1
    ways = ({"dom": rotated(dom, doms - 1, doms)}, {"dom": rotated(dom, 1, doms)})
    near = [{"shot": mine_out * inner + rotated(mine_in, r, inner)} for r in range(1, inner)]
    far = [{"shot": rotated(mine_out, r, outer) * inner + mine_in} for r in range(1, outer)]

    barrier = pltpu.get_barrier_semaphore()
    for there, way in zip((below, above), ways):

        @pl.when(there)
        def _():
            pl.semaphore_signal(barrier, inc=1, device_id=way, device_id_type=MESH)

    for peer in (*near, *far):
        pl.semaphore_signal(barrier, inc=1, device_id=peer, device_id_type=MESH)
    greeted = inner + outer - 2 + jnp.where(below, 1, 0) + jnp.where(above, 1, 0)

    def face_copy(step, half, side):
        return pltpu.make_async_remote_copy(
            src_ref=send_s.at[step, half, side, : 2 * COMP, :],
            dst_ref=recv_s.at[step, half, 1 - side, : 2 * COMP, :],
            send_sem=face_send.at[step, half, side],
            recv_sem=face_recv.at[step, half, 1 - side],
            device_id=ways[side],
            device_id_type=MESH,
        )

    now_s[...] = jnp.zeros(now_s.shape, F32)
    later_s[...] = jnp.zeros(later_s.shape, F32)
    src_s[...] = jnp.zeros(src_s.shape, F32)
    mass_s[...] = jnp.zeros(mass_s.shape, F32)
    force_s[...] = jnp.zeros(force_s.shape, F32)
    mod_s[...] = jnp.zeros(mod_s.shape, F32)
    gsend_s[...] = jnp.zeros(gsend_s.shape, F32)
    hi_s[...] = jnp.full(hi_s.shape, -1, jnp.int32)
    lo_s[...] = jnp.full(lo_s.shape, -1, jnp.int32)

    elems = conn_v.shape[1]
    slots = faces_v.shape[1]
    loads["conn"].wait()
    conn = conn_v[...]
    hi_s[:NPE, :elems] = lax.shift_right_logical(conn, 8)
    lo_s[:NPE, :elems] = lax.bitwise_and(conn, 255)
    loads["faces"].wait()
    loads["count"].wait()
    slot = lax.broadcasted_iota(jnp.int32, (1, EL), 1)
    for side in range(2):
        for q in range(FQ):
            width = min(EL, slots - q * EL)
            row = NPE + side * FQ + q
            face = faces_v[side : side + 1, q * EL : q * EL + width]
            inside = slot[:, :width] + q * EL < count_v[0:1, side : side + 1]
            hi_s[row : row + 1, :width] = jnp.where(inside, lax.shift_right_logical(face, 8), -1)
            lo_s[row : row + 1, :width] = jnp.where(inside, lax.bitwise_and(face, 255), -1)

    spot = lax.broadcasted_iota(jnp.int32, (LO, 2 * EL), 0)

    def build(m, carry):
        lanes = pl.ds(pl.multiple_of(m * 2 * EL, 2 * EL), 2 * EL)
        row = jnp.concatenate([lo_s[pl.ds(2 * m, 1), :], lo_s[pl.ds(2 * m + 1, 1), :]], axis=1)
        oh_s[:, lanes] = jnp.where(spot == row, 1.0, 0.0).astype(BF16)
        return carry

    lax.fori_loop(0, GROUPS // 2, build, 0, unroll=2)

    spans = [(hi, hi * LO, min(LO, nodes - hi * LO)) for hi in range(HI)]

    def fill(ref, half, block):
        for hi, at, width in spans:
            for c in range(COMP):
                row = hi * CH + 2 * c
                ref[half, row : row + 2, :width] = block[c, :, at : at + width].astype(F32)

    loads["fn"].wait()
    fill(now_s, 0, fn_v)
    loads["an"].wait()
    fill(now_s, 1, an_v)
    loads["stiff"].wait()
    loads["shear"].wait()
    loads["lame"].wait()
    mod_s[0:1, :elems] = shear_v[...]
    mod_s[1:2, :elems] = lame_v[...]

    near_copies = [
        pltpu.make_async_remote_copy(
            src_ref=gsend_s,
            dst_ref=gin_s.at[r],
            send_sem=in_send.at[r],
            recv_sem=in_recv.at[r],
            device_id=near[r - 1],
            device_id_type=MESH,
        )
        for r in range(1, inner)
    ]
    far_copies = [
        pltpu.make_async_remote_copy(
            src_ref=gmid_s,
            dst_ref=gout_s.at[r],
            send_sem=out_send.at[r],
            recv_sem=out_recv.at[r],
            device_id=far[r - 1],
            device_id_type=MESH,
        )
        for r in range(1, outer)
    ]

    def join(step, half):
        for side, there in enumerate((below, above)):

            @pl.when(there)
            def _():
                face_copy(step, half, 1 - side).wait_recv()

        for side in range(2):
            first = side * FQ
            lhsf_s[:, first * EL : (first + FQ) * EL] = place(
                rows_of(hi_s, NPE + first, FQ), recv_s[step, half, side]
            )
        joined = jnp.dot(lhsf_s[...], oht_s[NPE * EL : GROUPS * EL, :], preferred_element_type=F32)
        now_s[half] = now_s[half] - mass_s[...] * joined

    def advance(half):
        now = now_s[half]
        ahead = 2.0 * now - later_s[half] - mass_s[...] * made_s[...] + src_s[half]
        later_s[half] = now
        now_s[half] = ahead

    def write(half, out):
        for hi, at, width in spans:
            for c in range(COMP):
                row = hi * CH + 2 * c
                out[c, :, at : at + width] = now_s[half, row : row + 2, :width].astype(BF16)

    def turn_block(m):
        part = pl.ds(pl.multiple_of(m * 2 * EL, 2 * EL), 2 * EL)
        oht_s[part, :] = oh_s[:, part].T

    def gather(half, first):
        state = now_s[half].astype(BF16)

        def some(m, carry):
            lanes = pl.ds(pl.multiple_of(m * BATCH * EL, BATCH * EL), BATCH * EL)
            table = jnp.dot(state, oh_s[:, lanes], preferred_element_type=F32)
            for n in range(0, BATCH, WIDE):
                got = pick(rows_of(hi_s, m * BATCH + n, WIDE), table[:, n * EL : (n + WIDE) * EL])
                for k in range(WIDE):
                    at = pl.multiple_of((m * BATCH + n + k) * CH, CH)
                    gath_s[pl.ds(at, CH), :] = got[:, k * EL : (k + 1) * EL]
                if first:
                    for k in range(TURNS * n // BATCH, TURNS * (n + WIDE) // BATCH):
                        turn_block(m * TURNS + k)
            return carry

        lax.fori_loop(0, NPE // BATCH, some, 0)

    def multiply(half):
        for c in range(COMP):
            both = [gath_s[pl.ds(2 * c + s, NPE, stride=CH), :] for s in range(2)]
            gmat_s[c * NPE : (c + 1) * NPE, :] = jnp.concatenate(both, axis=1).astype(BF16)
        prod = jnp.dot(stiff_v[...], gmat_s[...], preferred_element_type=F32)
        shear = jnp.concatenate([mod_s[0:1, :]] * 2, axis=1)
        lame = jnp.concatenate([mod_s[1:2, :]] * 2, axis=1)
        total = shear * prod[:TILE] + lame * prod[TILE:]
        for c in range(COMP):
            for s in range(2):
                at = (2 * c + s) * NPE
                force_s[at : at + NPE, :] = total[c * NPE : (c + 1) * NPE, s * EL : (s + 1) * EL]

        @pl.when(half == 0)
        def _():
            prod_s[...] = prod

    def correlate():
        other = gmat_s[...].astype(F32)
        for p in range(2):
            both = jnp.sum(other * prod_s[p * TILE : (p + 1) * TILE, :], axis=0, keepdims=True)
            gsend_s[p : p + 1, :] = gsend_s[p : p + 1, :] + both[:, :EL] + both[:, EL:]

    def scatter(first):
        def spread(n):
            part = [force_s[pl.ds(n + k, CH, stride=NPE), :] for k in range(2)]
            return place(rows_of(hi_s, n, 2), jnp.concatenate(part, axis=1))

        lhs = jnp.concatenate([spread(n) for n in range(0, NPE, 2)], axis=1)
        if first:
            for m in range(TURNS * NPE // BATCH, GROUPS // 2):
                turn_block(m)
        made_s[...] = jnp.dot(lhs, oht_s[: NPE * EL, :], preferred_element_type=F32)

    def faces(step, half):
        table = jnp.dot(
            made_s[...].astype(BF16), oh_s[:, NPE * EL : GROUPS * EL], preferred_element_type=F32
        )
        for side in range(2):
            at = side * FQ
            got = pick(rows_of(hi_s, NPE + at, FQ), table[:, at * EL : (at + FQ) * EL])
            send_s[step, half, side] = got

    def late_loads():
        loads["fl"].wait()
        fill(later_s, 0, fl_v)
        loads["al"].wait()
        fill(later_s, 1, al_v)
        loads["mass"].wait()
        for hi, at, width in spans:
            part = mass_v[at : at + width]
            mass_s[hi * CH : (hi + 1) * CH, :width] = jnp.broadcast_to(part[None], (CH, width))
        loads["src"].wait()
        fill(src_s, 1, src_v)
        src_s[1] = src_s[1] * mass_s[...]

    def near_sum():
        for copy in near_copies:
            copy.wait()
        gin_s[0] = gsend_s[...]
        total = gin_s[mine_in]
        for i in range(1, inner):
            total = total + gin_s[rotated(mine_in, inner - i, inner)]
        gmid_s[...] = total
        for copy in far_copies:
            copy.start()

    def one(p, carry, first=False):
        step, half = (0, 0) if first else (lax.div(p, 2), lax.rem(p, 2))

        @pl.when(p >= 2)
        def _():
            join(step - 1, half)

        @pl.when(p < 2 * STEPS)
        def _():
            gather(half, first)
            multiply(half)

            @pl.when(half == 1)
            def _():
                correlate()

            @pl.when(p == 2 * STEPS - 1)
            def _():
                for copy in near_copies:
                    copy.start()

            scatter(first)
            faces(step, half)

            if first:
                pl.semaphore_wait(barrier, greeted)

            for side, there in enumerate((below, above)):

                @pl.when(there)
                def _():
                    face_copy(step, half, side).start()

            if first:
                late_loads()

            advance(half)

            @pl.when(p == 2 * STEPS - 1)
            def _():
                near_sum()

        return carry

    one(0, 0, True)
    lax.fori_loop(1, 2 * STEPS + 2, one, 0)
    write(0, fwd_ref)
    write(1, adj_ref)

    for copy in far_copies:
        copy.wait()
    gout_s[0] = gmid_s[...]
    total = gout_s[mine_out]
    for i in range(1, outer):
        total = total + gout_s[rotated(mine_out, outer - i, outer)]
    grad_ref[...] = (total * scale)[:2, :elems]
    for step in range(STEPS):
        for half in range(2):
            for side, there in enumerate((below, above)):

                @pl.when(there)
                def _():
                    face_copy(step, half, side).wait_send()


def put(fwd_ref, adj_ref, grad_ref, fwd_out, adj_out, grad_out, fwd_v, adj_v, grad_v, sem):
    rows = ((fwd_ref, fwd_v, fwd_out), (adj_ref, adj_v, adj_out), (grad_ref, grad_v, grad_out))
    ins = [pltpu.make_async_copy(a, v, sem.at[i]) for i, (a, v, b) in enumerate(rows)]
    outs = [pltpu.make_async_copy(v, b, sem.at[3 + i]) for i, (a, v, b) in enumerate(rows)]
    for copy in ins:
        copy.start()
    for copy, out in zip(ins, outs):
        copy.wait()
        out.start()
    for out in outs:
        out.wait()


def local(
    doms,
    shots,
    fwd_later,
    fwd_now,
    adj_later,
    adj_now,
    adj_src,
    mass_step,
    shear_mod,
    lame_mod,
    stiffness,
    conn,
    face_nodes,
    face_count,
):
    fields, comps, nodes = fwd_now.shape
    elems = conn.shape[0]
    inner = math.gcd(shots, 4)
    outer = shots // inner
    turn = lambda x: jnp.transpose(x, (1, 0, 2))
    scale = -1.0 / (16.0 * math.sqrt(fields * shots))
    dma = pltpu.SemaphoreType.DMA
    vmem = pltpu.VMEM
    body = functools.partial(kernel, doms, inner, outer, nodes, scale)
    operands = (
        turn(fwd_later),
        turn(fwd_now),
        turn(adj_later),
        turn(adj_now),
        turn(adj_src),
        mass_step,
        shear_mod[None],
        lame_mod[None],
        stiffness.reshape(2 * TILE, TILE),
        conn.T,
        face_nodes[0],
        face_count,
    )
    half = (2, HI * CH, LO)
    fwd, adj, grad = pl.pallas_call(
        body,
        out_shape=(
            jax.ShapeDtypeStruct((comps, fields, nodes), BF16),
            jax.ShapeDtypeStruct((comps, fields, nodes), BF16),
            jax.ShapeDtypeStruct((2, elems), F32),
        ),
        in_specs=[pl.BlockSpec(memory_space=pltpu.HBM)] * 12,
        out_specs=[pl.BlockSpec(memory_space=pltpu.VMEM)] * 3,
        scratch_shapes=[
            *[vmem(x.shape, x.dtype) for x in operands],
            dma((len(operands),)),
            vmem(half, F32),
            vmem(half, F32),
            vmem(half, F32),
            vmem(half[1:], F32),
            vmem((ROWS, EL), jnp.int32),
            vmem((ROWS, EL), jnp.int32),
            vmem((LO, GROUPS * EL), BF16),
            vmem((GROUPS * EL, LO), BF16),
            vmem((NPE * CH, EL), F32),
            vmem((TILE, 2 * EL), BF16),
            vmem((2 * TILE, 2 * EL), F32),
            vmem((CH * NPE, EL), F32),
            vmem((HI * CH, 2 * FQ * EL), BF16),
            vmem(half[1:], F32),
            vmem((STEPS, 2, 2, CH, FQ * EL), F32),
            vmem((STEPS, 2, 2, CH, FQ * EL), F32),
            vmem((8, EL), F32),
            vmem((8, EL), F32),
            vmem((inner, 8, EL), F32),
            vmem((8, EL), F32),
            vmem((outer, 8, EL), F32),
            dma((STEPS, 2, 2)),
            dma((STEPS, 2, 2)),
            dma((inner,)),
            dma((inner,)),
            dma((outer,)),
            dma((outer,)),
        ],
        compiler_params=pltpu.CompilerParams(
            collective_id=0, has_side_effects=True, vmem_limit_bytes=56 * 2**20
        ),
        name="fwi_window",
    )(*operands)
    whole = (fwd, adj, grad)
    fwd, adj, grad = pl.pallas_call(
        put,
        out_shape=tuple(jax.ShapeDtypeStruct(x.shape, x.dtype) for x in whole),
        in_specs=[pl.BlockSpec(memory_space=pl.ANY)] * 3,
        out_specs=[pl.BlockSpec(memory_space=pl.ANY)] * 3,
        scratch_shapes=[*[vmem(x.shape, x.dtype) for x in whole], dma((6,))],
        compiler_params=pltpu.CompilerParams(vmem_limit_bytes=56 * 2**20),
        name="results",
    )(*whole)
    return turn(fwd), turn(adj), grad


def solution(mesh):
    in_specs = (
        P("shot", None, "dom"),
        P("shot", None, "dom"),
        P("shot", None, "dom"),
        P("shot", None, "dom"),
        P("shot", None, "dom"),
        P("dom"),
        P("dom"),
        P("dom"),
        P(),
        P("dom", None),
        P("dom", None, None),
        P("dom", None),
    )
    out_specs = (P("shot", None, "dom"), P("shot", None, "dom"), P(None, "dom"))
    return jax.shard_map(
        functools.partial(local, mesh.shape["dom"], mesh.shape["shot"]),
        mesh=mesh,
        in_specs=in_specs,
        out_specs=out_specs,
        check_vma=False,
    )
```

```python
import functools
import math

import jax
import jax.numpy as jnp
from jax import lax
from jax.experimental import pallas as pl
from jax.experimental.pallas import tpu as pltpu
from jax.sharding import PartitionSpec as P

STEPS = 2
COMP = 3
NPE = 64
TILE = 192
CH = 8
LO = 256
HI = 16
EL = 128
FQ = 5
GROUPS = NPE + 2 * FQ
ROWS = 80
WIDE = 8
BATCH = 32
TURNS = 9
F32 = jnp.float32
BF16 = jnp.bfloat16
MESH = pl.DeviceIdType.MESH


def rotated(me, step, size):
    return lax.rem(me + step, size)


def rows_of(ref, first, count):
    return jnp.concatenate(
        [jnp.broadcast_to(ref[pl.ds(first + k, 1), :], (CH, EL)) for k in range(count)], axis=1
    )


def pick(rows, table):
    out = table[:CH]
    for hi in range(1, HI):
        out = jnp.where(rows == hi, table[hi * CH : (hi + 1) * CH], out)
    return out


def place(rows, part):
    return jnp.concatenate([jnp.where(rows == hi, part, 0.0) for hi in range(HI)], axis=0).astype(BF16)


def kernel(
    doms,
    inner,
    outer,
    nodes,
    scale,
    fl_h,
    fn_h,
    al_h,
    an_h,
    src_h,
    mass_h,
    shear_h,
    lame_h,
    stiff_h,
    conn_h,
    faces_h,
    count_h,
    fwd_ref,
    adj_ref,
    grad_ref,
    fl_v,
    fn_v,
    al_v,
    an_v,
    src_v,
    mass_v,
    shear_v,
    lame_v,
    stiff_v,
    conn_v,
    faces_v,
    count_v,
    load_sem,
    now_s,
    later_s,
    src_s,
    mass_s,
    hi_s,
    lo_s,
    oh_s,
    oht_s,
    gath_s,
    gmat_s,
    prod_s,
    force_s,
    lhsf_s,
    made_s,
    send_s,
    recv_s,
    mod_s,
    gsend_s,
    gin_s,
    gmid_s,
    gout_s,
    face_send,
    face_recv,
    in_send,
    in_recv,
    out_send,
    out_recv,
):
    names = ("conn", "faces", "count", "fn", "an", "stiff", "shear", "lame", "fl", "al", "mass", "src")
    from_hbm = (conn_h, faces_h, count_h, fn_h, an_h, stiff_h, shear_h, lame_h, fl_h, al_h, mass_h, src_h)
    to_vmem = (conn_v, faces_v, count_v, fn_v, an_v, stiff_v, shear_v, lame_v, fl_v, al_v, mass_v, src_v)
    loads = {
        name: pltpu.make_async_copy(a, b, load_sem.at[i])
        for i, (name, a, b) in enumerate(zip(names, from_hbm, to_vmem))
    }
    for load in loads.values():
        load.start()

    dom = lax.axis_index("dom")
    shot = lax.axis_index("shot")
    mine_in = lax.rem(shot, inner)
    mine_out = lax.div(shot, inner)
    below = dom > 0
    above = dom < doms - 1
    ways = ({"dom": rotated(dom, doms - 1, doms)}, {"dom": rotated(dom, 1, doms)})
    near = [{"shot": mine_out * inner + rotated(mine_in, r, inner)} for r in range(1, inner)]
    far = [{"shot": rotated(mine_out, r, outer) * inner + mine_in} for r in range(1, outer)]

    barrier = pltpu.get_barrier_semaphore()
    for there, way in zip((below, above), ways):

        @pl.when(there)
        def _():
            pl.semaphore_signal(barrier, inc=1, device_id=way, device_id_type=MESH)

    for peer in (*near, *far):
        pl.semaphore_signal(barrier, inc=1, device_id=peer, device_id_type=MESH)
    greeted = inner + outer - 2 + jnp.where(below, 1, 0) + jnp.where(above, 1, 0)

    def face_copy(step, half, side):
        return pltpu.make_async_remote_copy(
            src_ref=send_s.at[step, half, side, : 2 * COMP, :],
            dst_ref=recv_s.at[step, half, 1 - side, : 2 * COMP, :],
            send_sem=face_send.at[step, half, side],
            recv_sem=face_recv.at[step, half, 1 - side],
            device_id=ways[side],
            device_id_type=MESH,
        )

    now_s[...] = jnp.zeros(now_s.shape, F32)
    later_s[...] = jnp.zeros(later_s.shape, F32)
    src_s[...] = jnp.zeros(src_s.shape, F32)
    mass_s[...] = jnp.zeros(mass_s.shape, F32)
    force_s[...] = jnp.zeros(force_s.shape, F32)
    mod_s[...] = jnp.zeros(mod_s.shape, F32)
    gsend_s[...] = jnp.zeros(gsend_s.shape, F32)
    hi_s[...] = jnp.full(hi_s.shape, -1, jnp.int32)
    lo_s[...] = jnp.full(lo_s.shape, -1, jnp.int32)

    elems = conn_v.shape[1]
    slots = faces_v.shape[1]
    loads["conn"].wait()
    conn = conn_v[...]
    hi_s[:NPE, :elems] = lax.shift_right_logical(conn, 8)
    lo_s[:NPE, :elems] = lax.bitwise_and(conn, 255)
    loads["faces"].wait()
    loads["count"].wait()
    slot = lax.broadcasted_iota(jnp.int32, (1, EL), 1)
    for side in range(2):
        for q in range(FQ):
            width = min(EL, slots - q * EL)
            row = NPE + side * FQ + q
            face = faces_v[side : side + 1, q * EL : q * EL + width]
            inside = slot[:, :width] + q * EL < count_v[0:1, side : side + 1]
            hi_s[row : row + 1, :width] = jnp.where(inside, lax.shift_right_logical(face, 8), -1)
            lo_s[row : row + 1, :width] = jnp.where(inside, lax.bitwise_and(face, 255), -1)

    spot = lax.broadcasted_iota(jnp.int32, (LO, 2 * EL), 0)

    def build(m, carry):
        lanes = pl.ds(pl.multiple_of(m * 2 * EL, 2 * EL), 2 * EL)
        row = jnp.concatenate([lo_s[pl.ds(2 * m, 1), :], lo_s[pl.ds(2 * m + 1, 1), :]], axis=1)
        oh_s[:, lanes] = jnp.where(spot == row, 1.0, 0.0).astype(BF16)
        return carry

    lax.fori_loop(0, GROUPS // 2, build, 0, unroll=2)

    spans = [(hi, hi * LO, min(LO, nodes - hi * LO)) for hi in range(HI)]

    def fill(ref, half, block):
        for hi, at, width in spans:
            for c in range(COMP):
                row = hi * CH + 2 * c
                ref[half, row : row + 2, :width] = block[c, :, at : at + width].astype(F32)

    loads["fn"].wait()
    fill(now_s, 0, fn_v)
    loads["an"].wait()
    fill(now_s, 1, an_v)
    loads["stiff"].wait()
    loads["shear"].wait()
    loads["lame"].wait()
    mod_s[0:1, :elems] = shear_v[...]
    mod_s[1:2, :elems] = lame_v[...]

    near_copies = [
        pltpu.make_async_remote_copy(
            src_ref=gsend_s,
            dst_ref=gin_s.at[r],
            send_sem=in_send.at[r],
            recv_sem=in_recv.at[r],
            device_id=near[r - 1],
            device_id_type=MESH,
        )
        for r in range(1, inner)
    ]
    far_copies = [
        pltpu.make_async_remote_copy(
            src_ref=gmid_s,
            dst_ref=gout_s.at[r],
            send_sem=out_send.at[r],
            recv_sem=out_recv.at[r],
            device_id=far[r - 1],
            device_id_type=MESH,
        )
        for r in range(1, outer)
    ]

    def join(step, half):
        for side, there in enumerate((below, above)):

            @pl.when(there)
            def _():
                face_copy(step, half, 1 - side).wait_recv()

        for side in range(2):
            first = side * FQ
            lhsf_s[:, first * EL : (first + FQ) * EL] = place(
                rows_of(hi_s, NPE + first, FQ), recv_s[step, half, side]
            )
        joined = jnp.dot(lhsf_s[...], oht_s[NPE * EL : GROUPS * EL, :], preferred_element_type=F32)
        now_s[half] = now_s[half] - mass_s[...] * joined

    def advance(half):
        now = now_s[half]
        ahead = 2.0 * now - later_s[half] - mass_s[...] * made_s[...] + src_s[half]
        later_s[half] = now
        now_s[half] = ahead

    def write(half, out):
        for hi, at, width in spans:
            for c in range(COMP):
                row = hi * CH + 2 * c
                out[c, :, at : at + width] = now_s[half, row : row + 2, :width].astype(BF16)

    def turn_block(m):
        part = pl.ds(pl.multiple_of(m * 2 * EL, 2 * EL), 2 * EL)
        oht_s[part, :] = oh_s[:, part].T

    def gather(half, first):
        state = now_s[half].astype(BF16)

        def some(m, carry):
            lanes = pl.ds(pl.multiple_of(m * BATCH * EL, BATCH * EL), BATCH * EL)
            table = jnp.dot(state, oh_s[:, lanes], preferred_element_type=F32)
            for n in range(0, BATCH, WIDE):
                got = pick(rows_of(hi_s, m * BATCH + n, WIDE), table[:, n * EL : (n + WIDE) * EL])
                for k in range(WIDE):
                    at = pl.multiple_of((m * BATCH + n + k) * CH, CH)
                    gath_s[pl.ds(at, CH), :] = got[:, k * EL : (k + 1) * EL]
                if first:
                    for k in range(TURNS * n // BATCH, TURNS * (n + WIDE) // BATCH):
                        turn_block(m * TURNS + k)
            return carry

        lax.fori_loop(0, NPE // BATCH, some, 0)

    def multiply(half):
        for c in range(COMP):
            both = [gath_s[pl.ds(2 * c + s, NPE, stride=CH), :] for s in range(2)]
            gmat_s[c * NPE : (c + 1) * NPE, :] = jnp.concatenate(both, axis=1).astype(BF16)
        prod = jnp.dot(stiff_v[...], gmat_s[...], preferred_element_type=F32)
        shear = jnp.concatenate([mod_s[0:1, :]] * 2, axis=1)
        lame = jnp.concatenate([mod_s[1:2, :]] * 2, axis=1)
        total = shear * prod[:TILE] + lame * prod[TILE:]
        for c in range(COMP):
            for s in range(2):
                at = (2 * c + s) * NPE
                force_s[at : at + NPE, :] = total[c * NPE : (c + 1) * NPE, s * EL : (s + 1) * EL]

        @pl.when(half == 0)
        def _():
            prod_s[...] = prod

    def correlate():
        other = gmat_s[...].astype(F32)
        for p in range(2):
            both = jnp.sum(other * prod_s[p * TILE : (p + 1) * TILE, :], axis=0, keepdims=True)
            gsend_s[p : p + 1, :] = gsend_s[p : p + 1, :] + both[:, :EL] + both[:, EL:]

    def scatter(first):
        def spread(n):
            part = [force_s[pl.ds(n + k, CH, stride=NPE), :] for k in range(2)]
            return place(rows_of(hi_s, n, 2), jnp.concatenate(part, axis=1))

        lhs = jnp.concatenate([spread(n) for n in range(0, NPE, 2)], axis=1)
        if first:
            for m in range(TURNS * NPE // BATCH, GROUPS // 2):
                turn_block(m)
        made_s[...] = jnp.dot(lhs, oht_s[: NPE * EL, :], preferred_element_type=F32)

    def faces(step, half):
        table = jnp.dot(
            made_s[...].astype(BF16), oh_s[:, NPE * EL : GROUPS * EL], preferred_element_type=F32
        )
        for side in range(2):
            at = side * FQ
            got = pick(rows_of(hi_s, NPE + at, FQ), table[:, at * EL : (at + FQ) * EL])
            send_s[step, half, side] = got

            @pl.when((below, above)[side])
            def _():
                face_copy(step, half, side).start()

    def late_loads():
        loads["fl"].wait()
        fill(later_s, 0, fl_v)
        loads["al"].wait()
        fill(later_s, 1, al_v)
        loads["mass"].wait()
        for hi, at, width in spans:
            part = mass_v[at : at + width]
            mass_s[hi * CH : (hi + 1) * CH, :width] = jnp.broadcast_to(part[None], (CH, width))
        loads["src"].wait()
        fill(src_s, 1, src_v)
        src_s[1] = src_s[1] * mass_s[...]

    def near_sum():
        for copy in near_copies:
            copy.wait()
        gin_s[0] = gsend_s[...]
        total = gin_s[mine_in]
        for i in range(1, inner):
            total = total + gin_s[rotated(mine_in, inner - i, inner)]
        gmid_s[...] = total
        for copy in far_copies:
            copy.start()

    def one(p, carry, first=False):
        step, half = (0, 0) if first else (lax.div(p, 2), lax.rem(p, 2))

        @pl.when(p >= 2)
        def _():
            join(step - 1, half)

        @pl.when(p == 2 * STEPS)
        def _():
            near_sum()

        @pl.when(p < 2 * STEPS)
        def _():
            gather(half, first)
            multiply(half)

            @pl.when(half == 1)
            def _():
                correlate()

            @pl.when(p == 2 * STEPS - 1)
            def _():
                for copy in near_copies:
                    copy.start()

            scatter(first)
            if first:
                pl.semaphore_wait(barrier, greeted)
            faces(step, half)

            if first:
                late_loads()

            advance(half)

        return carry

    one(0, 0, True)
    lax.fori_loop(1, 2 * STEPS + 2, one, 0)
    write(0, fwd_ref)
    write(1, adj_ref)

    for copy in far_copies:
        copy.wait()
    gout_s[0] = gmid_s[...]
    total = gout_s[mine_out]
    for i in range(1, outer):
        total = total + gout_s[rotated(mine_out, outer - i, outer)]
    grad_ref[...] = (total * scale)[:2, :elems]
    for step in range(STEPS):
        for half in range(2):
            for side, there in enumerate((below, above)):

                @pl.when(there)
                def _():
                    face_copy(step, half, side).wait_send()


def put(fwd_ref, adj_ref, grad_ref, fwd_out, adj_out, grad_out, fwd_v, adj_v, grad_v, sem):
    rows = ((fwd_ref, fwd_v, fwd_out), (adj_ref, adj_v, adj_out), (grad_ref, grad_v, grad_out))
    ins = [pltpu.make_async_copy(a, v, sem.at[i]) for i, (a, v, b) in enumerate(rows)]
    outs = [pltpu.make_async_copy(v, b, sem.at[3 + i]) for i, (a, v, b) in enumerate(rows)]
    for copy in ins:
        copy.start()
    for copy, out in zip(ins, outs):
        copy.wait()
        out.start()
    for out in outs:
        out.wait()


def local(
    doms,
    shots,
    fwd_later,
    fwd_now,
    adj_later,
    adj_now,
    adj_src,
    mass_step,
    shear_mod,
    lame_mod,
    stiffness,
    conn,
    face_nodes,
    face_count,
):
    fields, comps, nodes = fwd_now.shape
    elems = conn.shape[0]
    inner = math.gcd(shots, 4)
    outer = shots // inner
    turn = lambda x: jnp.transpose(x, (1, 0, 2))
    scale = -1.0 / (16.0 * math.sqrt(fields * shots))
    dma = pltpu.SemaphoreType.DMA
    vmem = pltpu.VMEM
    body = functools.partial(kernel, doms, inner, outer, nodes, scale)
    operands = (
        turn(fwd_later),
        turn(fwd_now),
        turn(adj_later),
        turn(adj_now),
        turn(adj_src),
        mass_step,
        shear_mod[None],
        lame_mod[None],
        stiffness.reshape(2 * TILE, TILE),
        conn.T,
        face_nodes[0],
        face_count,
    )
    half = (2, HI * CH, LO)
    fwd, adj, grad = pl.pallas_call(
        body,
        out_shape=(
            jax.ShapeDtypeStruct((comps, fields, nodes), BF16),
            jax.ShapeDtypeStruct((comps, fields, nodes), BF16),
            jax.ShapeDtypeStruct((2, elems), F32),
        ),
        in_specs=[pl.BlockSpec(memory_space=pltpu.HBM)] * 12,
        out_specs=[pl.BlockSpec(memory_space=pltpu.VMEM)] * 3,
        scratch_shapes=[
            *[vmem(x.shape, x.dtype) for x in operands],
            dma((len(operands),)),
            vmem(half, F32),
            vmem(half, F32),
            vmem(half, F32),
            vmem(half[1:], F32),
            vmem((ROWS, EL), jnp.int32),
            vmem((ROWS, EL), jnp.int32),
            vmem((LO, GROUPS * EL), BF16),
            vmem((GROUPS * EL, LO), BF16),
            vmem((NPE * CH, EL), F32),
            vmem((TILE, 2 * EL), BF16),
            vmem((2 * TILE, 2 * EL), F32),
            vmem((CH * NPE, EL), F32),
            vmem((HI * CH, 2 * FQ * EL), BF16),
            vmem(half[1:], F32),
            vmem((STEPS, 2, 2, CH, FQ * EL), F32),
            vmem((STEPS, 2, 2, CH, FQ * EL), F32),
            vmem((8, EL), F32),
            vmem((8, EL), F32),
            vmem((inner, 8, EL), F32),
            vmem((8, EL), F32),
            vmem((outer, 8, EL), F32),
            dma((STEPS, 2, 2)),
            dma((STEPS, 2, 2)),
            dma((inner,)),
            dma((inner,)),
            dma((outer,)),
            dma((outer,)),
        ],
        compiler_params=pltpu.CompilerParams(
            collective_id=0, has_side_effects=True, vmem_limit_bytes=56 * 2**20
        ),
        name="fwi_window",
    )(*operands)
    whole = (fwd, adj, grad)
    fwd, adj, grad = pl.pallas_call(
        put,
        out_shape=tuple(jax.ShapeDtypeStruct(x.shape, x.dtype) for x in whole),
        in_specs=[pl.BlockSpec(memory_space=pl.ANY)] * 3,
        out_specs=[pl.BlockSpec(memory_space=pl.ANY)] * 3,
        scratch_shapes=[*[vmem(x.shape, x.dtype) for x in whole], dma((6,))],
        compiler_params=pltpu.CompilerParams(vmem_limit_bytes=56 * 2**20),
        name="results",
    )(*whole)
    return turn(fwd), turn(adj), grad


def solution(mesh):
    in_specs = (
        P("shot", None, "dom"),
        P("shot", None, "dom"),
        P("shot", None, "dom"),
        P("shot", None, "dom"),
        P("shot", None, "dom"),
        P("dom"),
        P("dom"),
        P("dom"),
        P(),
        P("dom", None),
        P("dom", None, None),
        P("dom", None),
    )
    out_specs = (P("shot", None, "dom"), P("shot", None, "dom"), P(None, "dom"))
    return jax.shard_map(
        functools.partial(local, mesh.shape["dom"], mesh.shape["shot"]),
        mesh=mesh,
        in_specs=in_specs,
        out_specs=out_specs,
        check_vma=False,
    )
```
